32 devices in a mesh: pairs: 2 (over y), rows: 8 (over z, x), cols: 2 (over core).
Axes of the slice: x: 2, y: 2, z: 4, core: 2. Of those that a mesh axis runs over, the one named last changes fastest.
Arguments:
- left_image: bfloat16 [32, 1024, 128], P(('pairs', 'rows'), 'cols'), parts along dimension 0, may hold values from -6 to 6
- right_image: bfloat16 [32, 1024, 128], P(('pairs', 'rows'), 'cols'), parts along dimension 0, may hold values from -6 to 6
- weight: bfloat16 [1152, 256], replicated, may hold values from -0.1875 to 0.1875
- level_zero: bfloat16 [32, 1024, 256], P(('pairs', 'rows'), 'cols'), parts along dimension 0, may hold values from -6 to 6
- level_one: bfloat16 [32, 1024, 128], P(('pairs', 'rows'), 'cols'), parts along dimension 0, may hold values from -6 to 6
- level_two: bfloat16 [32, 1024, 64], P(('pairs', 'rows'), 'cols'), parts along dimension 0, may hold values from -6 to 6
- level_three: bfloat16 [32, 1024, 32], P(('pairs', 'rows'), 'cols'), parts along dimension 0, may hold values from -6 to 6
Outputs:
- grad_left_in: bfloat16 [32, 1024, 128], P(('pairs', 'rows'), 'cols'), parts along dimension 0
- grad_right_in: bfloat16 [32, 1024, 128], P(('pairs', 'rows'), 'cols'), parts along dimension 0
- weight_grad: float32 [512, 1152], P(('pairs', 'rows')), parts along dimension 0
The draws below stay inside these ranges and needn't reach their ends.
There are 2 independent parts, one for each index of `pairs`. The reference program is written for one: setup_inputs(seed, part) draws one part's arguments, and reference() takes and returns one part's arrays. A program takes and returns all parts, laid end to end along the dimension named above; an argument that names none is the same for every part. Nothing has to cross between parts.
All inputs are finite; a program needn't handle non-finite values.
Results may differ from the reference program's by a relative error of at most 0.008.
Values may be sent and summed in bfloat16 or wider, within the bound.
No kernel may reach another device: no remote copies, remote signals or barrier semaphores. Data moves between devices by JAX's collectives and lax.ppermute only.
A program may use at most 64 MiB of HBM per device.

```python
import math
import jax
import jax.numpy as jnp

DISP = 256
C = 256
CIN = 128
H = 16
W = 1024


def block_levels(key, dims, shards, low, high):
    def one(axis_at, parts):
        steps = jax.random.uniform(jax.random.fold_in(jax.random.fold_in(key, 6), axis_at), (parts,), jnp.float32, low / len(shards), high / len(shards))
        return jnp.repeat(jnp.exp(steps), dims[axis_at] // parts).reshape((-1,) + (1,) * (len(dims) - axis_at - 1))

    factor_of = one(*shards[0])
    for cut in shards[1:]:
        factor_of = factor_of * one(*cut)
    return factor_of


def scatter_about(stream_key, dims, deviation, reach, cuts=(), dtype=jnp.bfloat16):
    array = deviation * jax.random.normal(stream_key, dims, jnp.float32)
    if cuts:
        array = array * block_levels(stream_key, dims, cuts, -0.22, 0.18)
    return jnp.clip(array, -reach, reach).astype(dtype)


def setup_inputs(seed: int = 0, part: int = 0) -> dict:
    seeds = jax.random.split(jax.random.key(seed), 8)
    own_keys = jax.random.split(jax.random.fold_in(seeds[7], part), 8)
    left_image = scatter_about(own_keys[0], (H, W, CIN), 1.0, 6.0, ((0, 8), (1, 2)))
    right_image = scatter_about(own_keys[1], (H, W, CIN), 1.0, 6.0, ((0, 8), (1, 2)))
    weight = scatter_about(seeds[2], (9 * CIN, C), (9 * CIN) ** -0.5, 0.1875)
    level_zero = scatter_about(own_keys[3], (H, W, DISP), 1.0, 6.0, ((0, 8), (1, 2)))
    level_one = scatter_about(own_keys[4], (H, W, DISP // 2), 1.0, 6.0, ((0, 8), (1, 2)))
    level_two = scatter_about(own_keys[5], (H, W, DISP // 4), 1.0, 6.0, ((0, 8), (1, 2)))
    level_three = scatter_about(own_keys[6], (H, W, DISP // 8), 1.0, 6.0, ((0, 8), (1, 2)))
    return dict(left_image=left_image, right_image=right_image, weight=weight, level_zero=level_zero, level_one=level_one, level_two=level_two, level_three=level_three)


def skewed(band_rev):
    depth, count, width = band_rev.shape
    padded = jnp.pad(band_rev, ((0, 0), (0, 0), (0, count)))
    flat = padded.reshape(depth, count * (width + count))[:, :count * (width + count - 1)]
    return flat.reshape(depth, count, width + count - 1)

def combined_grad(level_zero, level_one, level_two, level_three):
    total = level_zero.astype(jnp.float32)
    total = total + jnp.repeat(level_one.astype(jnp.float32), 2, axis=-1) * 0.5
    total = total + jnp.repeat(level_two.astype(jnp.float32), 4, axis=-1) * 0.25
    total = total + jnp.repeat(level_three.astype(jnp.float32), 8, axis=-1) * 0.125
    return total.astype(jnp.bfloat16)

def reference(left_image, right_image, weight, level_zero, level_one, level_two, level_three):
    images = jnp.stack([left_image, right_image])
    framed = jnp.pad(images, ((0, 0), (1, 1), (1, 1), (0, 0)))
    out_sum = jnp.zeros((2 * H * W, C), jnp.float32)
    for row_tap in range(3):
        for col_tap in range(3):
            index = row_tap * 3 + col_tap
            taken = framed[:, row_tap:row_tap + H, col_tap:col_tap + W].reshape(-1, CIN)
            out_sum = out_sum + jnp.dot(taken, weight[index * CIN:(index + 1) * CIN], preferred_element_type=jnp.float32)
    feats = out_sum.astype(jnp.bfloat16).reshape(2, H, W, C)
    left_feat = feats[0]
    right_feat = feats[1]
    corr_grad = combined_grad(level_zero, level_one, level_two, level_three)
    edge = DISP - 1
    right_ext = jnp.pad(right_feat, ((0, 0), (edge, 0), (0, 0)))
    ext_grad = jnp.zeros((H, W + edge, C), jnp.float32)
    lefts = []
    for start in range(0, W, DISP):
        matrix = skewed(corr_grad[:, start:start + DISP, ::-1]).astype(jnp.float32)
        window = right_ext[:, start:start + DISP + edge].astype(jnp.float32)
        lefts.append(jnp.einsum('rik,rkc->ric', matrix, window))
        block_left = left_feat[:, start:start + DISP].astype(jnp.float32)
        ext_grad = ext_grad.at[:, start:start + DISP + edge].add(jnp.einsum('rik,ric->rkc', matrix, block_left))
    inverse = 1.0 / math.sqrt(C)
    left_grad = (jnp.concatenate(lefts, axis=1) * inverse).astype(jnp.bfloat16)
    right_grad = (ext_grad[:, edge:] * inverse).astype(jnp.bfloat16)
    feat_grad = jnp.stack([left_grad, right_grad])
    bordered = jnp.pad(feat_grad, ((0, 0), (1, 1), (1, 1), (0, 0)))
    flat_grad = feat_grad.reshape(-1, C)
    back_sum = jnp.zeros((2 * H * W, CIN), jnp.float32)
    pieces = []
    for row_tap in range(3):
        for col_tap in range(3):
            index = row_tap * 3 + col_tap
            taps_w = weight[index * CIN:(index + 1) * CIN]
            shifted = bordered[:, 2 - row_tap:2 - row_tap + H, 2 - col_tap:2 - col_tap + W].reshape(-1, C)
            back_sum = back_sum + jnp.dot(shifted, taps_w.T, preferred_element_type=jnp.float32)
            taken = framed[:, row_tap:row_tap + H, col_tap:col_tap + W].reshape(-1, CIN)
            pieces.append(jnp.dot(flat_grad.T, taken, preferred_element_type=jnp.float32))
    grad_pair = back_sum.astype(jnp.bfloat16).reshape(2, H, W, CIN)
    scale = 1.0 / math.sqrt(2 * H * W)
    weight_grad = jnp.concatenate(pieces, axis=1) * scale
    return (grad_pair[0], grad_pair[1], weight_grad)
```

```python
import math

import jax
import jax.numpy as jnp
from jax import lax
from jax.experimental import pallas as pl
from jax.experimental.pallas import tpu as pltpu
from jax.sharding import PartitionSpec as P

BF = jnp.bfloat16
F32 = jnp.float32
MIB = 1 << 20
PAD = 8


def dot(a, b):
    return jnp.dot(a, b, preferred_element_type=F32)


def vmem(count):
    return [pl.BlockSpec(memory_space=pltpu.VMEM)] * count


SCALAR = pl.BlockSpec(memory_space=pltpu.SMEM)


def shape(dims, dtype):
    return jax.ShapeDtypeStruct(dims, dtype)


def params(mib):
    return pltpu.CompilerParams(vmem_limit_bytes=mib * MIB)


def payload_kernel(core, left, right, own, near, sems):
    c = core[0]
    copies = []
    for target, row in ((own, c), (near, 1 - c)):
        for image, source in enumerate((left, right)):
            copies.append(
                pltpu.make_async_copy(source.at[row], target.at[image], sems.at[len(copies)])
            )
    for copy in copies:
        copy.start()
    for copy in copies:
        copy.wait()


def levels_kernel(core, zero, one, two, three, keep, send):
    c = core[0]
    reach = zero.shape[2]

    def spread(factor):
        source = lax.broadcasted_iota(jnp.int32, (reach // factor, reach), 0)
        target = lax.broadcasted_iota(jnp.int32, (reach // factor, reach), 1)
        first = source * factor
        inside = (target >= first) & (target < first + factor)
        return jnp.where(inside, 1.0 / factor, 0.0).astype(BF)

    a = lax.broadcasted_iota(jnp.int32, (reach, reach), 0)
    b = lax.broadcasted_iota(jnp.int32, (reach, reach), 1)
    mirror = jnp.where(a + b == reach - 1, 1.0, 0.0).astype(BF)
    for target, row in ((keep, c), (send, 1 - c)):
        total = zero[row].astype(F32)
        total = total + dot(one[row], spread(2))
        total = total + dot(two[row], spread(4))
        total = total + dot(three[row], spread(8))
        target[...] = dot(total.astype(BF), mirror).astype(BF)


def shifted_3(scratch, size):
    return jnp.concatenate(
        [scratch[pl.ds(PAD + by, size)].astype(BF) for by in (-1, 0, 1)], axis=1
    )


def clear_pads(scratch, size):
    zeros = jnp.zeros((PAD, scratch.shape[1]), F32)
    scratch[pl.ds(0, PAD)] = zeros
    scratch[pl.ds(PAD + size, PAD)] = zeros


def prepare_kernel(
    core, left, right, left_got, right_got, corr, corr_got, weight,
    own_sum, images_t, band, band_t, taps, padded, rows,
):
    c = core[0]
    half = left.shape[1]
    size = 2 * half
    channels = left.shape[2]
    features = weight.shape[2]
    reach = corr.shape[1]
    here = pl.multiple_of(c * half, half)
    there = pl.multiple_of((1 - c) * half, half)
    inner_tap = 2 - 2 * c
    outer_tap = 2 * c
    clear_pads(padded, size)
    for image, (mine, got) in enumerate(((left, left_got), (right, right_got))):
        total = None
        for role, (row, tap) in enumerate(((c, 1), (1 - c, inner_tap))):
            padded[pl.ds(PAD + here, half)] = mine[row].astype(F32)
            padded[pl.ds(PAD + there, half)] = got[row].astype(F32)
            images_t[image, pl.ds(role * channels, channels)] = (
                padded[pl.ds(PAD, size)].T.astype(BF)
            )
            part = dot(shifted_3(padded, size), weight[tap])
            total = part if total is None else total + part
        own_sum[image] = total
    rows[pl.ds(here, half)] = corr[...]
    rows[pl.ds(there, half)] = corr_got[...]
    for block in range(size // reach):
        values = rows[pl.ds(block * reach, reach)].astype(F32)
        wide = jnp.concatenate([values, jnp.zeros_like(values)], axis=1)
        skewed = pltpu.roll(wide, 1, 1, stride=1, stride_axis=0)
        band[block] = skewed.astype(BF)
        band_t[block] = skewed.T.astype(BF)
    for place, tap in enumerate((outer_tap, 1, inner_tap)):
        for col in range(3):
            piece = weight[tap, pl.ds(col * channels, channels)].astype(F32)
            taps[pl.ds(col * features, features), pl.ds(place * channels, channels)] = (
                piece.T.astype(BF)
            )


def main_kernel(
    core, halo_same, halo_other, weight, own_sum, images_t, band, band_t, taps,
    edge_same, edge_other, wg_keep, wg_send, in_keep, in_send,
    padded, feats, wide, grads, wg,
):
    c = core[0]
    half = halo_same.shape[1]
    size = 2 * half
    channels = halo_same.shape[2]
    features = feats.shape[2]
    blocks, reach = band.shape[0], band.shape[1]
    here = pl.multiple_of(c * half, half)
    there = pl.multiple_of((1 - c) * half, half)
    outer_tap = 2 * c
    inverse = 1.0 / math.sqrt(features)
    clear_pads(padded, size)
    clear_pads(wide, size)
    halo_t = []
    for image in range(2):
        padded[pl.ds(PAD + here, half)] = halo_same[image].astype(F32)
        padded[pl.ds(PAD + there, half)] = halo_other[image].astype(F32)
        halo_t.append(padded[pl.ds(PAD, size)].T.astype(BF))
        feats[image] = (
            own_sum[image] + dot(shifted_3(padded, size), weight[outer_tap])
        ).astype(BF)
    for image in range(2):
        for block in range(blocks):
            low = pl.ds(block * reach, reach)
            if image == 0:
                total = dot(band[block, :, pl.ds(reach, reach)], feats[1, low])
                if block:
                    total = total + dot(
                        band[block, :, pl.ds(0, reach)], feats[1, pl.ds((block - 1) * reach, reach)]
                    )
            else:
                total = dot(band_t[block, pl.ds(reach, reach)], feats[0, low])
                if block + 1 < blocks:
                    total = total + dot(
                        band_t[block + 1, pl.ds(0, reach)],
                        feats[0, pl.ds((block + 1) * reach, reach)],
                    )
            wide[pl.ds(PAD + block * reach, reach)] = total * inverse
        for index, by in enumerate((1, 0, -1)):
            grads[image, :, pl.ds(index * features, features)] = (
                wide[pl.ds(PAD + by, size)].astype(BF)
            )
        edge = dot(grads[image], taps[:, pl.ds(0, channels)])
        padded[pl.ds(PAD, size)] = edge
        edge_same[image] = padded[pl.ds(PAD + here, half)].astype(BF)
        edge_other[image] = padded[pl.ds(PAD + there, half)].astype(BF)
    for image in range(2):
        both = dot(grads[image], taps[:, pl.ds(channels, 2 * channels)])
        for role, row in ((0, c), (1, 1 - c)):
            padded[pl.ds(PAD, size)] = both[:, role * channels : (role + 1) * channels]
            in_keep[image, row] = padded[pl.ds(PAD + here, half)].astype(in_keep.dtype)
            in_send[image, row] = padded[pl.ds(PAD + there, half)].astype(BF)
    inner = None
    outer = None
    for image in range(2):
        part = dot(images_t[image], grads[image])
        inner = part if inner is None else inner + part
        part = dot(halo_t[image], grads[image])
        outer = part if outer is None else outer + part
    own_wg = inner[:channels].T
    inner_wg = inner[channels:].T
    outer_wg = outer.T
    first = c == 0
    wg[:, pl.ds(0, channels)] = jnp.where(first, outer_wg, inner_wg)
    wg[:, pl.ds(channels, channels)] = own_wg
    wg[:, pl.ds(2 * channels, channels)] = jnp.where(first, inner_wg, outer_wg)
    if wg_keep.shape == wg.shape:
        wg_keep[...] = wg[...]
        return
    chunks = wg_keep.shape[0]
    piece = features // chunks // 2
    for col in range(3):
        for chunk in range(chunks):
            start = col * features + chunk * 2 * piece
            rows = pl.ds(col * piece, piece)
            wg_keep[chunk, rows] = wg[
                pl.ds(pl.multiple_of(start + c * piece, piece), piece)
            ].astype(wg_keep.dtype)
            wg_send[chunk, rows] = wg[
                pl.ds(pl.multiple_of(start + (1 - c) * piece, piece), piece)
            ].astype(wg_send.dtype)


def add_kernel(keep, got, out):
    out[...] = (keep[...].astype(F32) + got[...].astype(F32)).astype(BF)


def sum_kernel(scale, parts, out):
    total = parts[0].astype(F32)
    for index in range(1, parts.shape[0]):
        total = total + parts[index].astype(F32)
    out[...] = total * scale


def finish_weight_kernel(core, mine, got, out):
    c = core[0]
    piece = mine.shape[0] // 3
    channels = mine.shape[1] // 3
    for source, place in ((mine, c), (got, 1 - c)):
        rows = pl.ds(pl.multiple_of(place * piece, piece), piece)
        for tap in range(3):
            for col in range(3):
                out[rows, pl.ds((tap * 3 + col) * channels, channels)] = source[
                    pl.ds(col * piece, piece), pl.ds(tap * channels, channels)
                ]


def finish_kernel(core, keep, got, edge_same, edge_other, left, right):
    c = core[0]
    for image, out in enumerate((left, right)):
        for row, edge in ((c, edge_other), (1 - c, edge_same)):
            out[row] = (
                keep[image, row].astype(F32)
                + got[image, row].astype(F32)
                + edge[image].astype(F32)
            ).astype(BF)


def on_device(left_image, right_image, weight, level_zero, level_one, level_two, level_three):
    depth, band, channels = left_image.shape
    features = weight.shape[1]
    reach = level_zero.shape[2]
    cores = lax.axis_size("cols")
    chips = lax.axis_size("rows")
    size = band * cores
    blocks = size // reach
    core = lax.axis_index("cols").astype(jnp.int32).reshape(1)
    swap = [(i, cores - 1 - i) for i in range(cores)]
    same_in, same_out, other = [], [], []
    for chip in range(chips - 1):
        low = chip * cores
        high = low + cores
        same_in += [(low, high), (high + 1, low + 1)]
        same_out += [(high, low), (low + 1, high + 1)]
        other += [(low + 1, high), (high, low + 1)]
    flat = ("rows", "cols")

    row_shape = shape((2, band, channels), BF)
    pay_other, pay_same = pl.pallas_call(
        payload_kernel,
        out_shape=(row_shape, row_shape),
        in_specs=[SCALAR] + [pl.BlockSpec(memory_space=pl.ANY)] * 2,
        out_specs=[pl.BlockSpec(memory_space=pl.ANY)] * 2,
        scratch_shapes=[pltpu.SemaphoreType.DMA((4,))],
    )(core, left_image, right_image)
    halo_other = lax.ppermute(pay_other, flat, other)
    halo_same = lax.ppermute(pay_same, flat, same_in)
    left_got = lax.ppermute(left_image, "cols", swap)
    right_got = lax.ppermute(right_image, "cols", swap)

    corr, corr_send = pl.pallas_call(
        levels_kernel,
        out_shape=(shape((band, reach), BF),) * 2,
        in_specs=[SCALAR] + vmem(4),
        out_specs=vmem(2),
        compiler_params=params(16),
    )(core, level_zero, level_one, level_two, level_three)
    corr_got = lax.ppermute(corr_send, "cols", swap)

    weight_3 = weight.reshape(3, 3 * channels, features)
    own_sum, images_t, skew, skew_t, taps = pl.pallas_call(
        prepare_kernel,
        out_shape=(
            shape((2, size, features), F32),
            shape((2, 2 * channels, size), BF),
            shape((blocks, reach, 2 * reach), BF),
            shape((blocks, 2 * reach, reach), BF),
            shape((3 * features, 3 * channels), BF),
        ),
        in_specs=[SCALAR] + vmem(7),
        out_specs=vmem(5),
        scratch_shapes=[
            pltpu.VMEM((size + 2 * PAD, channels), F32),
            pltpu.VMEM((size, reach), BF),
        ],
        compiler_params=params(32),
    )(core, left_image, right_image, left_got, right_got, corr, corr_got, weight_3)

    piece = features // chips // cores
    tiled = piece % 16 == 0
    wg_shape = (chips, 3 * piece, 3 * channels)
    wg_outs = (shape(wg_shape, F32), shape(wg_shape, BF))
    if not tiled:
        wg_outs = (shape((3 * features, 3 * channels), F32), shape((16, 128), BF))
    edge_same, edge_other, wg_keep, wg_send, in_keep, in_send = pl.pallas_call(
        main_kernel,
        out_shape=(
            row_shape,
            row_shape,
            *wg_outs,
            shape((2, depth, band, channels), F32),
            shape((2, depth, band, channels), BF),
        ),
        in_specs=[SCALAR] + vmem(8),
        out_specs=vmem(6),
        scratch_shapes=[
            pltpu.VMEM((size + 2 * PAD, channels), F32),
            pltpu.VMEM((2, size, features), BF),
            pltpu.VMEM((size + 2 * PAD, features), F32),
            pltpu.VMEM((2, size, 3 * features), BF),
            pltpu.VMEM((3 * features, 3 * channels), F32),
        ],
        compiler_params=params(40),
    )(core, halo_same, halo_other, weight_3, own_sum, images_t, skew, skew_t, taps)

    got_other = lax.ppermute(edge_other, flat, other)
    got_same = lax.ppermute(edge_same, flat, same_out)
    if not tiled:
        halves = wg_keep.reshape(3, chips, cores, piece, 3 * channels).transpose(2, 1, 0, 3, 4)
        halves = halves.reshape(cores, *wg_shape)
        wg_keep = lax.dynamic_index_in_dim(halves, core[0], 0, False)
        wg_send = lax.dynamic_index_in_dim(halves, cores - 1 - core[0], 0, False).astype(BF)
    wg_got = lax.ppermute(wg_send, "cols", swap)
    in_got = lax.ppermute(in_send, "cols", swap)
    chip_wg = pl.pallas_call(
        add_kernel,
        out_shape=shape(wg_send.shape, BF),
        in_specs=vmem(2),
        out_specs=vmem(1)[0],
        compiler_params=params(16),
    )(wg_keep, wg_got)
    parts = lax.all_to_all(chip_wg, "rows", 0, 0, tiled=False)
    scale = 1.0 / math.sqrt(2 * depth * band * chips * cores)
    mine = pl.pallas_call(
        lambda *refs: sum_kernel(scale, *refs),
        out_shape=shape(wg_send.shape[1:], F32),
        in_specs=vmem(1),
        out_specs=vmem(1)[0],
        compiler_params=params(16),
    )(parts)
    theirs = lax.ppermute(mine, "cols", swap)
    if tiled:
        weight_grad = pl.pallas_call(
            finish_weight_kernel,
            out_shape=shape((2 * piece, 9 * channels), F32),
            in_specs=[SCALAR] + vmem(2),
            out_specs=vmem(1)[0],
            compiler_params=params(16),
        )(core, mine, theirs)
    else:
        first = core[0] == 0
        both = jnp.stack([jnp.where(first, mine, theirs), jnp.where(first, theirs, mine)])
        both = both.reshape(cores, 3, piece, 3, channels).transpose(0, 2, 3, 1, 4)
        weight_grad = both.reshape(cores * piece, 9 * channels)
    grad_left, grad_right = pl.pallas_call(
        finish_kernel,
        out_shape=(shape(left_image.shape, BF),) * 2,
        in_specs=[SCALAR] + vmem(4),
        out_specs=vmem(2),
        compiler_params=params(16),
    )(core, in_keep, in_got, got_same, got_other)
    return grad_left, grad_right, weight_grad


def solution(mesh):
    block = P(("pairs", "rows"), "cols", None)
    return jax.shard_map(
        on_device,
        mesh=mesh,
        in_specs=(block, block, P(), block, block, block, block),
        out_specs=(block, block, P(("pairs", "rows"), None)),
        check_vma=False,
    )
```

```python
import functools
import math

import jax
import jax.numpy as jnp
from jax import lax
from jax.experimental import pallas as pl
from jax.experimental.pallas import tpu as pltpu
from jax.sharding import PartitionSpec as P

BF = jnp.bfloat16
F32 = jnp.float32
MIB = 1 << 20
PAD = 8


def dot(a, b):
    return jnp.dot(a, b, preferred_element_type=F32)


def vmem(count):
    return [pl.BlockSpec(memory_space=pltpu.VMEM)] * count


SCALAR = pl.BlockSpec(memory_space=pltpu.SMEM)


def shape(dims, dtype):
    return jax.ShapeDtypeStruct(dims, dtype)


SMALL = pl.CostEstimate(flops=1, bytes_accessed=1, transcendentals=0)


LARGE = pl.CostEstimate(flops=10**11, bytes_accessed=1, transcendentals=0)


def params(mib):
    return pltpu.CompilerParams(vmem_limit_bytes=mib * MIB)


def first_kernel(core, left, right, own, near, sems):
    c = core[0]
    copies = []
    for target, row in ((own, c), (near, 1 - c)):
        for image, source in enumerate((left, right)):
            copies.append(
                pltpu.make_async_copy(source.at[row], target.at[image], sems.at[len(copies)])
            )
    for copy in copies:
        copy.start()
    for copy in copies:
        copy.wait()


def spread(factor, reach):
    source = lax.broadcasted_iota(jnp.int32, (reach // factor, reach), 0)
    target = lax.broadcasted_iota(jnp.int32, (reach // factor, reach), 1)
    first = source * factor
    inside = (target >= first) & (target < first + factor)
    return jnp.where(inside, 1.0 / factor, 0.0).astype(BF)


def mirrored(zero, one, two_t, three_t):
    reach = zero.shape[1]
    a = lax.broadcasted_iota(jnp.int32, (reach, reach), 0)
    b = lax.broadcasted_iota(jnp.int32, (reach, reach), 1)
    mirror = jnp.where(a + b == reach - 1, 1.0, 0.0).astype(BF)
    total = zero.astype(F32)
    total = total + dot(one, spread(2, reach))
    total = total + dot(two_t.astype(F32).T.astype(BF), spread(4, reach))
    total = total + dot(three_t.astype(F32).T.astype(BF), spread(8, reach))
    return dot(total.astype(BF), mirror).astype(BF)


def shifted_3(scratch, size):
    return jnp.concatenate(
        [scratch[pl.ds(PAD + by, size)].astype(BF) for by in (-1, 0, 1)], axis=1
    )


def clear_pads(scratch, size):
    zeros = jnp.zeros((PAD, scratch.shape[1]), F32)
    scratch[pl.ds(0, PAD)] = zeros
    scratch[pl.ds(PAD + size, PAD)] = zeros


def started(moves, sems):
    copies = [
        pltpu.make_async_copy(source, target, sems.at[index])
        for index, (source, target) in enumerate(moves)
    ]
    for copy in copies:
        copy.start()
    return copies


def local_kernel(
    core, weight_hbm, zero_hbm, one_hbm, two_hbm, three_hbm,
    corr, taps, outer_weight,
    weight, zero, one, two, three, sems,
):
    c = core[0]
    copies = started(
        (
            (weight_hbm, weight),
            (zero_hbm.at[c], zero),
            (one_hbm.at[c], one),
            (two_hbm.at[c], two),
            (three_hbm.at[c], three),
        ),
        sems,
    )
    features = weight.shape[2]
    channels = weight.shape[1] // 3
    copies[0].wait()
    for place, tap in enumerate((2 * c, 1, 2 - 2 * c)):
        for col in range(3):
            piece = weight[tap, pl.ds(col * channels, channels)].astype(F32)
            taps[pl.ds(col * features, features), pl.ds(place * channels, channels)] = (
                piece.T.astype(BF)
            )
    outer_weight[...] = weight[2 * c]
    for copy in copies[1:]:
        copy.wait()
    corr[...] = mirrored(zero[...], one[...], two[...], three[...])


def prepare_kernel(
    core, left, right, left_got, right_got, zero_got, one_got, two_got, three_got, weight_hbm,
    corr,
    own_sum, images_t, band, band_t,
    padded, rows, images, weight, zero, one, two, three, sems,
):
    c = core[0]
    half = left.shape[1]
    size = 2 * half
    channels = left.shape[2]
    reach = corr.shape[1]
    here = pl.multiple_of(c * half, half)
    there = pl.multiple_of((1 - c) * half, half)
    moves = [
        (zero_got.at[c], zero),
        (one_got.at[c], one),
        (two_got.at[c], two),
        (three_got.at[c], three),
    ]
    for image, (mine, got) in enumerate(((left, left_got), (right, right_got))):
        for role, row in enumerate((c, 1 - c)):
            moves.append((mine.at[row], images.at[image, role, pl.ds(here, half)]))
            moves.append((got.at[row], images.at[image, role, pl.ds(there, half)]))
    moves.append((weight_hbm, weight))
    copies = started(moves, sems)
    clear_pads(padded, size)
    rows[pl.ds(here, half)] = corr[...]
    for copy in copies[:4]:
        copy.wait()
    rows[pl.ds(there, half)] = mirrored(zero[...], one[...], two[...], three[...])
    for copy in copies[4:]:
        copy.wait()
    for image in range(2):
        total = None
        for role, tap in enumerate((1, 2 - 2 * c)):
            whole = images[image, role].astype(F32)
            padded[pl.ds(PAD, size)] = whole
            images_t[image, pl.ds(role * channels, channels)] = whole.T.astype(BF)
            part = dot(shifted_3(padded, size), weight[tap])
            total = part if total is None else total + part
        own_sum[image] = total
    for block in range(size // reach):
        values = rows[pl.ds(block * reach, reach)].astype(F32)
        wide = jnp.concatenate([values, jnp.zeros_like(values)], axis=1)
        skewed = pltpu.roll(wide, 1, 1, stride=1, stride_axis=0)
        band[block] = skewed.astype(BF)
        band_t[block] = skewed.T.astype(BF)


def at_end(chips, chip, upper):
    return chip == jnp.where(upper, chips - 1, 0)


def main_kernel(
    chips, core, chip, halo_same, halo_other, weight, own_sum, images_t, band, band_t, taps,
    whole_grad, edge_same, edge_other, wg_keep, across,
    padded, feats, wide, grads, wg, edges, pair, edge_sems,
):
    c = core[0]
    half = halo_same.shape[1]
    size = 2 * half
    channels = halo_same.shape[2]
    features = feats.shape[2]
    blocks, reach = band.shape[0], band.shape[1]
    here = pl.multiple_of(c * half, half)
    there = pl.multiple_of((1 - c) * half, half)
    inverse = 1.0 / math.sqrt(features)
    alone = at_end(chips, chip[0], c == 1)
    clear_pads(padded, size)
    clear_pads(wide, size)
    halo_t = []
    for image in range(2):
        for place, halo in ((here, halo_same), (there, halo_other)):
            padded[pl.ds(PAD + place, half)] = jnp.where(alone, 0.0, halo[image].astype(F32))
        halo_t.append(padded[pl.ds(PAD, size)].T.astype(BF))
        feats[image] = (
            own_sum[image] + dot(shifted_3(padded, size), weight[...])
        ).astype(BF)
    for image in range(2):
        for block in range(blocks):
            low = pl.ds(block * reach, reach)
            if image == 0:
                total = dot(band[block, :, pl.ds(reach, reach)], feats[1, low])
                if block:
                    total = total + dot(
                        band[block, :, pl.ds(0, reach)], feats[1, pl.ds((block - 1) * reach, reach)]
                    )
            else:
                total = dot(band_t[block, pl.ds(reach, reach)], feats[0, low])
                if block + 1 < blocks:
                    total = total + dot(
                        band_t[block + 1, pl.ds(0, reach)],
                        feats[0, pl.ds((block + 1) * reach, reach)],
                    )
            wide[pl.ds(PAD + block * reach, reach)] = total * inverse
        for index, by in enumerate((1, 0, -1)):
            grads[image, :, pl.ds(index * features, features)] = (
                wide[pl.ds(PAD + by, size)].astype(BF)
            )
        whole_grad[image] = grads[image, :, pl.ds(features, features)]
        padded[pl.ds(PAD, size)] = dot(grads[image], taps[:, pl.ds(0, channels)])
        for index, (place, out) in enumerate(((here, edge_same), (there, edge_other))):
            edges[index, image] = padded[pl.ds(PAD + place, half)].astype(BF)
            pltpu.make_async_copy(
                edges.at[index, image], out.at[image], edge_sems.at[2 * image + index]
            ).start()
    inner = None
    outer = None
    for image in range(2):
        part = dot(images_t[image], grads[image])
        inner = part if inner is None else inner + part
        part = dot(halo_t[image], grads[image])
        outer = part if outer is None else outer + part
    for image in range(2):
        for index, out in enumerate((edge_same, edge_other)):
            pltpu.make_async_copy(
                edges.at[index, image], out.at[image], edge_sems.at[2 * image + index]
            ).wait()
    own_wg = inner[:channels].T
    inner_wg = inner[channels:].T
    outer_wg = outer.T
    first = c == 0
    wg[:, pl.ds(0, channels)] = jnp.where(first, outer_wg, inner_wg)
    wg[:, pl.ds(channels, channels)] = own_wg
    wg[:, pl.ds(2 * channels, channels)] = jnp.where(first, inner_wg, outer_wg)
    for image in range(2):
        pair[...] = dot(grads[image], taps[:, pl.ds(channels, 2 * channels)])
        for role, row in ((0, c), (1, 1 - c)):
            lanes = pl.ds(role * channels, channels)
            across[2 * image + row] = pair[pl.ds(there, half), lanes].astype(BF)
    if wg_keep.shape == wg.shape:
        wg_keep[...] = wg[...]
        return
    chunks = wg_keep.shape[0]
    piece = features // chunks // 2
    for col in range(3):
        for chunk in range(chunks):
            start = col * features + chunk * 2 * piece
            wg_keep[chunk, pl.ds(col * piece, piece)] = wg[
                pl.ds(pl.multiple_of(start + c * piece, piece), piece)
            ]
            other = wg[pl.ds(pl.multiple_of(start + (1 - c) * piece, piece), piece)].astype(BF)
            for tap in range(3):
                across[4 + tap, pl.ds((chunk * 3 + col) * piece, piece)] = (
                    other[:, tap * channels : (tap + 1) * channels]
                )


def add_kernel(keep, across, out):
    chunks, rows, lanes = keep.shape
    for chunk in range(chunks):
        for tap in range(3):
            part = pl.ds(tap * lanes // 3, lanes // 3)
            out[chunk, :, part] = (
                keep[chunk, :, part] + across[4 + tap, pl.ds(chunk * rows, rows)].astype(F32)
            ).astype(BF)


def sum_kernel(scale, parts, _, out):
    total = parts[0].astype(F32)
    for index in range(1, parts.shape[0]):
        total = total + parts[index].astype(F32)
    out[...] = total * scale


def finish_weight_kernel(core, mine, got, out):
    c = core[0]
    piece = mine.shape[0] // 3
    channels = mine.shape[1] // 3
    for source, place in ((mine, c), (got, 1 - c)):
        rows = pl.ds(pl.multiple_of(place * piece, piece), piece)
        for tap in range(3):
            for col in range(3):
                out[rows, pl.ds((tap * 3 + col) * channels, channels)] = source[
                    pl.ds(col * piece, piece), pl.ds(tap * channels, channels)
                ]


def finish_kernel(
    chips, core, chip, whole_grad, taps, across, edge_same, edge_other,
    left, right, token,
    wide, part,
):
    c = core[0]
    half, channels = left.shape[1], left.shape[2]
    size = whole_grad.shape[1]
    here = pl.multiple_of(c * half, half)
    other_alone = at_end(chips, chip[0], c == 1)
    same_alone = at_end(chips, chip[0], c == 0)
    clear_pads(wide, size)
    for image, out in enumerate((left, right)):
        wide[pl.ds(PAD, size)] = whole_grad[image].astype(F32)
        part[...] = wide[pl.ds(here, half + 2 * PAD)]
        grads = jnp.concatenate(
            [part[pl.ds(PAD + by, half)].astype(BF) for by in (1, 0, -1)], axis=1
        )
        pair = dot(grads, taps[:, pl.ds(channels, 2 * channels)])
        for role, row, edge, alone in (
            (0, c, edge_other, other_alone),
            (1, 1 - c, edge_same, same_alone),
        ):
            out[row] = (
                pair[:, role * channels : (role + 1) * channels]
                + across[2 * image + row].astype(F32)
                + jnp.where(alone, 0.0, edge[image].astype(F32))
            ).astype(BF)
    token[...] = jnp.zeros_like(token)


def on_device(left_image, right_image, weight, level_zero, level_one, level_two, level_three):
    depth, band, channels = left_image.shape
    features = weight.shape[1]
    reach = level_zero.shape[2]
    cores = lax.axis_size("cols")
    chips = lax.axis_size("rows")
    size = band * cores
    blocks = size // reach
    core = lax.axis_index("cols").astype(jnp.int32).reshape(1)
    chip_at = lax.axis_index("rows").astype(jnp.int32).reshape(1)
    swap = [(i, cores - 1 - i) for i in range(cores)]
    parts_count = lax.axis_size("pairs")
    flat = ("pairs", "rows", "cols")
    same_in, same_out, other = [], [], []
    for part in range(parts_count):
        base = part * chips * cores
        for chip in range(chips - 1):
            low = base + chip * cores
            high = low + cores
            same_in += [(low, high), (high + 1, low + 1)]
            same_out += [(high, low), (low + 1, high + 1)]
            other += [(low + 1, high), (high, low + 1)]
        first = base
        last = base + (chips - 1) * cores
        same_in += [(last, last + 1), (first + 1, first)]
        same_out += [(last + 1, last), (first, first + 1)]
        across = (part ^ 1) if parts_count % 2 == 0 else part
        away = (across - part) * chips * cores
        other += [(first, first + away), (last + 1, last + 1 + away)]

    row_shape = shape((2, band, channels), BF)
    params_in = (
        left_image,
        right_image,
        level_zero,
        level_one,
        level_two.transpose(0, 2, 1),
        level_three.transpose(0, 2, 1),
        weight.reshape(3, 3 * channels, features),
    )
    in_hbm = [pltpu.with_memory_space_constraint(x, pltpu.HBM) for x in params_in]
    any_space = pl.BlockSpec(memory_space=pl.ANY)
    own, near = pl.pallas_call(
        first_kernel,
        out_shape=(row_shape, row_shape),
        in_specs=[SCALAR] + [any_space] * 2,
        out_specs=vmem(2),
        scratch_shapes=[pltpu.SemaphoreType.DMA((4,))],
        cost_estimate=SMALL,
        compiler_params=params(2),
    )(core, *in_hbm[:2])
    halo_other = lax.ppermute(own, flat, other)
    halo_same = lax.ppermute(near, flat, same_in)
    from_core = lax.optimization_barrier((own, *params_in))[1:]
    got = [
        pltpu.with_memory_space_constraint(lax.ppermute(x, "cols", swap), pltpu.HBM)
        for x in from_core[:6]
    ]

    corr, taps, outer_weight = pl.pallas_call(
        local_kernel,
        out_shape=(
            shape((band, reach), BF),
            shape((3 * features, 3 * channels), BF),
            shape((3 * channels, features), BF),
        ),
        in_specs=[SCALAR] + [any_space] * 5,
        out_specs=vmem(3),
        scratch_shapes=[
            pltpu.VMEM((3, 3 * channels, features), BF),
            pltpu.VMEM((band, reach), BF),
            pltpu.VMEM((band, reach // 2), BF),
            pltpu.VMEM((reach // 4, band), BF),
            pltpu.VMEM((reach // 8, band), BF),
            pltpu.SemaphoreType.DMA((5,)),
        ],
        cost_estimate=LARGE,
        compiler_params=params(8),
    )(core, in_hbm[6], *in_hbm[2:6])
    own_sum, images_t, skew, skew_t = pl.pallas_call(
        prepare_kernel,
        out_shape=(
            shape((2, size, features), F32),
            shape((2, 2 * channels, size), BF),
            shape((blocks, reach, 2 * reach), BF),
            shape((blocks, 2 * reach, reach), BF),
        ),
        in_specs=[SCALAR] + [any_space] * 9 + vmem(1),
        out_specs=vmem(4),
        scratch_shapes=[
            pltpu.VMEM((size + 2 * PAD, channels), F32),
            pltpu.VMEM((size, reach), BF),
            pltpu.VMEM((2, 2, size, channels), BF),
            pltpu.VMEM((3, 3 * channels, features), BF),
            pltpu.VMEM((band, reach), BF),
            pltpu.VMEM((band, reach // 2), BF),
            pltpu.VMEM((reach // 4, band), BF),
            pltpu.VMEM((reach // 8, band), BF),
            pltpu.SemaphoreType.DMA((13,)),
        ],
        cost_estimate=SMALL,
        compiler_params=params(12),
    )(core, *in_hbm[:2], *got, in_hbm[6], corr)

    piece = features // chips // cores
    tiled = piece % 16 == 0
    wg_shape = (chips, 3 * piece, 3 * channels)
    wg_out = shape(wg_shape if tiled else (3 * features, 3 * channels), F32)
    across_shape = (7 if tiled else 4, max(band, 3 * piece * chips), channels)
    whole_grad, edge_same, edge_other, wg_keep, across = pl.pallas_call(
        functools.partial(main_kernel, chips),
        out_shape=(
            shape((2, size, features), BF),
            pltpu.HBM(row_shape.shape, BF),
            pltpu.HBM(row_shape.shape, BF),
            wg_out,
            shape(across_shape, BF),
        ),
        in_specs=[SCALAR] * 2 + vmem(8),
        out_specs=vmem(1) + [any_space] * 2 + vmem(2),
        scratch_shapes=[
            pltpu.VMEM((size + 2 * PAD, channels), F32),
            pltpu.VMEM((2, size, features), BF),
            pltpu.VMEM((size + 2 * PAD, features), F32),
            pltpu.VMEM((2, size, 3 * features), BF),
            pltpu.VMEM((3 * features, 3 * channels), F32),
            pltpu.VMEM((2, *row_shape.shape), BF),
            pltpu.VMEM((size, 2 * channels), F32),
            pltpu.SemaphoreType.DMA((4,)),
        ],
        cost_estimate=SMALL,
        compiler_params=params(16),
    )(core, chip_at, halo_same, halo_other, outer_weight, own_sum, images_t, skew, skew_t, taps)

    got_other = lax.ppermute(edge_other, flat, other)
    got_same = lax.ppermute(edge_same, flat, same_out)
    across_got = lax.ppermute(across, "cols", swap)
    if tiled:
        chip_wg = pl.pallas_call(
            add_kernel,
            out_shape=shape(wg_shape, BF),
            in_specs=vmem(2),
            out_specs=vmem(1)[0],
            cost_estimate=SMALL,
            compiler_params=params(4),
        )(wg_keep, across_got)
    else:
        halves = wg_keep.reshape(3, chips, cores, piece, 3 * channels).transpose(2, 1, 0, 3, 4)
        halves = halves.reshape(cores, *wg_shape)
        mine = lax.dynamic_index_in_dim(halves, core[0], 0, False)
        theirs = lax.dynamic_index_in_dim(halves, cores - 1 - core[0], 0, False).astype(BF)
        chip_wg = (mine + lax.ppermute(theirs, "cols", swap).astype(F32)).astype(BF)
    parts = lax.all_to_all(chip_wg, "rows", 0, 0, tiled=False)
    grad_left, grad_right, token = pl.pallas_call(
        functools.partial(finish_kernel, chips),
        out_shape=(shape(left_image.shape, BF),) * 2 + (shape((8, 128), F32),),
        in_specs=[SCALAR] * 2 + vmem(5),
        out_specs=vmem(3),
        scratch_shapes=[
            pltpu.VMEM((size + 2 * PAD, features), F32),
            pltpu.VMEM((band + 2 * PAD, features), F32),
        ],
        cost_estimate=LARGE,
        compiler_params=params(8),
    )(core, chip_at, whole_grad, taps, across_got, got_same, got_other)
    scale = 1.0 / math.sqrt(2 * depth * band * chips * cores)
    mine = pl.pallas_call(
        functools.partial(sum_kernel, scale),
        out_shape=shape(wg_shape[1:], F32),
        in_specs=vmem(2),
        out_specs=vmem(1)[0],
        cost_estimate=SMALL,
        compiler_params=params(4),
    )(parts, token)
    theirs = lax.ppermute(mine, "cols", swap)
    if tiled:
        weight_grad = pl.pallas_call(
            finish_weight_kernel,
            out_shape=shape((2 * piece, 9 * channels), F32),
            in_specs=[SCALAR] + vmem(2),
            out_specs=vmem(1)[0],
            cost_estimate=SMALL,
            compiler_params=params(4),
        )(core, mine, theirs)
    else:
        first = core[0] == 0
        both = jnp.stack([jnp.where(first, mine, theirs), jnp.where(first, theirs, mine)])
        both = both.reshape(cores, 3, piece, 3, channels).transpose(0, 2, 3, 1, 4)
        weight_grad = both.reshape(cores * piece, 9 * channels)
    return grad_left, grad_right, weight_grad


def solution(mesh):
    block = P(("pairs", "rows"), "cols", None)
    return jax.shard_map(
        on_device,
        mesh=mesh,
        in_specs=(block, block, P(), block, block, block, block),
        out_specs=(block, block, P(("pairs", "rows"), None)),
        check_vma=False,
    )
```

```python
import functools
import math

import jax
import jax.numpy as jnp
from jax import lax
from jax.experimental import pallas as pl
from jax.experimental.pallas import tpu as pltpu
from jax.sharding import PartitionSpec as P

BF = jnp.bfloat16
F32 = jnp.float32
MIB = 1 << 20
PAD = 8


def dot(a, b):
    return jnp.dot(a, b, preferred_element_type=F32)


def vmem(count):
    return [pl.BlockSpec(memory_space=pltpu.VMEM)] * count


SCALAR = pl.BlockSpec(memory_space=pltpu.SMEM)


def shape(dims, dtype):
    return jax.ShapeDtypeStruct(dims, dtype)


SMALL = pl.CostEstimate(flops=1, bytes_accessed=1, transcendentals=0)


LARGE = pl.CostEstimate(flops=10**11, bytes_accessed=1, transcendentals=0)


def params(mib):
    return pltpu.CompilerParams(vmem_limit_bytes=mib * MIB)


def started(moves, sems):
    copies = [
        pltpu.make_async_copy(source, target, sems.at[index])
        for index, (source, target) in enumerate(moves)
    ]
    for copy in copies:
        copy.start()
    return copies


def packed(source, target, first):
    count, lanes = source.shape[0], target.shape[1]
    moves = []
    for index in range(source.shape[1] // lanes):
        moves.append(
            (source.at[:, pl.ds(index * lanes, lanes)], target.at[pl.ds(first, count)])
        )
        first += count
    return moves, first


def level_moves(levels, pack, first):
    moves = []
    for level in levels:
        more, first = packed(level, pack, first)
        moves += more
    return moves


def first_kernel(
    core, left, right, zero, one, two, three,
    own, near, pack, sems,
):
    c = core[0]
    half = left.shape[1]
    moves = []
    for image, source in enumerate((left, right)):
        moves += [(source.at[c], own.at[image]), (source.at[1 - c], near.at[image])]
    for index, source in enumerate((left.at[c], left.at[1 - c], right.at[c], right.at[1 - c])):
        moves.append((source, pack.at[pl.ds(index * half, half)]))
    moves += level_moves([x.at[1 - c] for x in (zero, one, two, three)], pack, 4 * half)
    for copy in started(moves, sems):
        copy.wait()


def spread(factor, reach):
    source = lax.broadcasted_iota(jnp.int32, (reach // factor, reach), 0)
    target = lax.broadcasted_iota(jnp.int32, (reach // factor, reach), 1)
    first = source * factor
    inside = (target >= first) & (target < first + factor)
    return jnp.where(inside, 1.0 / factor, 0.0).astype(BF)


def mirrored(zero, one, two_t, three_t):
    reach = zero.shape[1]
    a = lax.broadcasted_iota(jnp.int32, (reach, reach), 0)
    b = lax.broadcasted_iota(jnp.int32, (reach, reach), 1)
    mirror = jnp.where(a + b == reach - 1, 1.0, 0.0).astype(BF)
    total = zero.astype(F32)
    total = total + dot(one, spread(2, reach))
    total = total + dot(two_t.astype(F32).T.astype(BF), spread(4, reach))
    total = total + dot(three_t.astype(F32).T.astype(BF), spread(8, reach))
    return dot(total.astype(BF), mirror).astype(BF)


def shifted_3(scratch, size, first=0):
    return jnp.concatenate(
        [scratch[pl.ds(PAD + first + by, size)].astype(BF) for by in (-1, 0, 1)], axis=1
    )


def clear_pads(scratch, size):
    zeros = jnp.zeros((PAD, scratch.shape[1]), F32)
    scratch[pl.ds(0, PAD)] = zeros
    scratch[pl.ds(PAD + size, PAD)] = zeros


def local_kernel(
    core, weight_hbm, zero_hbm, one_hbm, two_hbm, three_hbm,
    corr, taps,
    weight, zero, one, two, three, sems,
):
    c = core[0]
    copies = started(
        (
            (weight_hbm, weight),
            (zero_hbm.at[c], zero),
            (one_hbm.at[c], one),
            (two_hbm.at[c], two),
            (three_hbm.at[c], three),
        ),
        sems,
    )
    features = weight.shape[2]
    channels = weight.shape[1] // 3
    copies[0].wait()
    for place, tap in enumerate((2 * c, 1, 2 - 2 * c)):
        for col in range(3):
            piece = weight[tap, pl.ds(col * channels, channels)].astype(F32)
            taps[pl.ds(col * features, features), pl.ds(place * channels, channels)] = (
                piece.T.astype(BF)
            )
    for copy in copies[1:]:
        copy.wait()
    corr[...] = mirrored(zero[...], one[...], two[...], three[...])


def prepare_kernel(
    core, left, right, got, weight_hbm, corr,
    own_sum, images_t, band, band_t, outer_weight,
    padded, rows, images, weight, zero, one, two, three, sems,
):
    c = core[0]
    half = left.shape[1]
    size = 2 * half
    channels = left.shape[2]
    reach = corr.shape[1]
    here = pl.multiple_of(c * half, half)
    there = pl.multiple_of((1 - c) * half, half)
    moves = [(b, a) for a, b in level_moves((zero, one, two, three), got, 4 * half)]
    levels = len(moves)
    for image, mine in enumerate((left, right)):
        for role, row in enumerate((c, 1 - c)):
            block = 2 * image + 1 - role
            moves.append((mine.at[row], images.at[image, role, pl.ds(here, half)]))
            moves.append(
                (got.at[pl.ds(block * half, half)], images.at[image, role, pl.ds(there, half)])
            )
    moves.append((weight_hbm, weight))
    copies = started(moves, sems)
    clear_pads(padded, size)
    rows[pl.ds(here, half)] = corr[...]
    for copy in copies[:levels]:
        copy.wait()
    rows[pl.ds(there, half)] = mirrored(zero[...], one[...], two[...], three[...])
    for copy in copies[levels:]:
        copy.wait()
    for image in range(2):
        total = None
        for role, tap in enumerate((1, 2 - 2 * c)):
            whole = images[image, role].astype(F32)
            padded[pl.ds(PAD, size)] = whole
            images_t[image, pl.ds(role * channels, channels)] = whole.T.astype(BF)
            part = dot(shifted_3(padded, size), weight[tap])
            total = part if total is None else total + part
        own_sum[image] = total
    outer_weight[...] = weight[2 * c]
    for block in range(size // reach):
        values = rows[pl.ds(block * reach, reach)].astype(F32)
        wide = jnp.concatenate([values, jnp.zeros_like(values)], axis=1)
        skewed = pltpu.roll(wide, 1, 1, stride=1, stride_axis=0)
        band[block] = skewed.astype(BF)
        band_t[block] = skewed.T.astype(BF)


def at_end(chips, chip, upper):
    return chip == jnp.where(upper, chips - 1, 0)


def main_kernel(
    chips, core, chip, halo_same, halo_other, weight, own_sum, images_t, band, band_t, taps,
    whole_grad, edge_same, edge_other, wg_keep, across,
    padded, feats, wide, grads, wg, edges, edge_sems,
):
    c = core[0]
    half = halo_same.shape[1]
    size = 2 * half
    channels = halo_same.shape[2]
    features = feats.shape[2]
    blocks, reach = band.shape[0], band.shape[1]
    here = pl.multiple_of(c * half, half)
    there = pl.multiple_of((1 - c) * half, half)
    inverse = 1.0 / math.sqrt(features)
    alone = at_end(chips, chip[0], c == 1)
    clear_pads(padded, size)
    clear_pads(wide, size)
    halo_t = []
    for image in range(2):
        for place, halo in ((here, halo_same), (there, halo_other)):
            padded[pl.ds(PAD + place, half)] = jnp.where(alone, 0.0, halo[image].astype(F32))
        halo_t.append(padded[pl.ds(PAD, size)].T.astype(BF))
        for block in range(blocks):
            rows = pl.ds(block * reach, reach)
            part = dot(shifted_3(padded, reach, block * reach), weight[...])
            feats[image, rows] = (own_sum[image, rows] + part).astype(BF)
    for image in range(2):
        for block in range(blocks):
            low = pl.ds(block * reach, reach)
            if image == 0:
                total = dot(band[block, :, pl.ds(reach, reach)], feats[1, low])
                if block:
                    total = total + dot(
                        band[block, :, pl.ds(0, reach)], feats[1, pl.ds((block - 1) * reach, reach)]
                    )
            else:
                total = dot(band_t[block, pl.ds(reach, reach)], feats[0, low])
                if block + 1 < blocks:
                    total = total + dot(
                        band_t[block + 1, pl.ds(0, reach)],
                        feats[0, pl.ds((block + 1) * reach, reach)],
                    )
            wide[pl.ds(PAD + block * reach, reach)] = total * inverse
        for index, by in enumerate((1, 0, -1)):
            grads[image, :, pl.ds(index * features, features)] = (
                wide[pl.ds(PAD + by, size)].astype(BF)
            )
        whole_grad[image] = grads[image, :, pl.ds(features, features)]
        padded[pl.ds(PAD, size)] = dot(grads[image], taps[:, pl.ds(0, channels)])
        for index, (place, out) in enumerate(((here, edge_same), (there, edge_other))):
            edges[index, image] = padded[pl.ds(PAD + place, half)].astype(BF)
            pltpu.make_async_copy(
                edges.at[index, image], out.at[image], edge_sems.at[2 * image + index]
            ).start()
    inner = dot(images_t[0], grads[0]) + dot(images_t[1], grads[1])
    outer = dot(halo_t[0], grads[0]) + dot(halo_t[1], grads[1])
    for image in range(2):
        for index, out in enumerate((edge_same, edge_other)):
            pltpu.make_async_copy(
                edges.at[index, image], out.at[image], edge_sems.at[2 * image + index]
            ).wait()
    own_wg = inner[:channels].T
    inner_wg = inner[channels:].T
    outer_wg = outer.T
    first = c == 0
    wg[:, pl.ds(0, channels)] = jnp.where(first, outer_wg, inner_wg)
    wg[:, pl.ds(channels, channels)] = own_wg
    wg[:, pl.ds(2 * channels, channels)] = jnp.where(first, inner_wg, outer_wg)
    for image in range(2):
        pair = dot(grads[image, pl.ds(there, half)], taps[:, pl.ds(channels, 2 * channels)])
        for role, row in ((0, c), (1, 1 - c)):
            across[2 * image + row] = pair[:, role * channels : (role + 1) * channels].astype(BF)
    if wg_keep.shape == wg.shape:
        wg_keep[...] = wg[...]
        return
    chunks = wg_keep.shape[0]
    piece = features // chunks // 2
    for col in range(3):
        for chunk in range(chunks):
            start = col * features + chunk * 2 * piece
            wg_keep[chunk, pl.ds(col * piece, piece)] = wg[
                pl.ds(pl.multiple_of(start + c * piece, piece), piece)
            ]
            other = wg[pl.ds(pl.multiple_of(start + (1 - c) * piece, piece), piece)].astype(BF)
            for tap in range(3):
                across[4 + tap, pl.ds((chunk * 3 + col) * piece, piece)] = (
                    other[:, tap * channels : (tap + 1) * channels]
                )


def add_kernel(keep, across, out):
    chunks, rows, lanes = keep.shape
    for chunk in range(chunks):
        for tap in range(3):
            part = pl.ds(tap * lanes // 3, lanes // 3)
            out[chunk, :, part] = (
                keep[chunk, :, part] + across[4 + tap, pl.ds(chunk * rows, rows)].astype(F32)
            ).astype(BF)


def sum_kernel(scale, parts, _, out):
    total = parts[0].astype(F32)
    for index in range(1, parts.shape[0]):
        total = total + parts[index].astype(F32)
    out[...] = total * scale


def finish_weight_kernel(core, mine, got, out):
    c = core[0]
    piece = mine.shape[0] // 3
    channels = mine.shape[1] // 3
    for source, place in ((mine, c), (got, 1 - c)):
        rows = pl.ds(pl.multiple_of(place * piece, piece), piece)
        for tap in range(3):
            for col in range(3):
                out[rows, pl.ds((tap * 3 + col) * channels, channels)] = source[
                    pl.ds(col * piece, piece), pl.ds(tap * channels, channels)
                ]


def finish_kernel(
    chips, core, chip, whole_grad, taps, across, edge_same, edge_other,
    left, right, token,
    wide, part,
):
    c = core[0]
    half, channels = left.shape[1], left.shape[2]
    size = whole_grad.shape[1]
    here = pl.multiple_of(c * half, half)
    other_alone = at_end(chips, chip[0], c == 1)
    same_alone = at_end(chips, chip[0], c == 0)
    clear_pads(wide, size)
    for image, out in enumerate((left, right)):
        wide[pl.ds(PAD, size)] = whole_grad[image].astype(F32)
        part[...] = wide[pl.ds(here, half + 2 * PAD)]
        grads = jnp.concatenate(
            [part[pl.ds(PAD + by, half)].astype(BF) for by in (1, 0, -1)], axis=1
        )
        pair = dot(grads, taps[:, pl.ds(channels, 2 * channels)])
        for role, row, edge, alone in (
            (0, c, edge_other, other_alone),
            (1, 1 - c, edge_same, same_alone),
        ):
            out[row] = (
                pair[:, role * channels : (role + 1) * channels]
                + across[2 * image + row].astype(F32)
                + jnp.where(alone, 0.0, edge[image].astype(F32))
            ).astype(BF)
    token[...] = jnp.zeros_like(token)


def on_device(left_image, right_image, weight, level_zero, level_one, level_two, level_three):
    depth, band, channels = left_image.shape
    features = weight.shape[1]
    reach = level_zero.shape[2]
    cores = lax.axis_size("cols")
    chips = lax.axis_size("rows")
    size = band * cores
    blocks = size // reach
    core = lax.axis_index("cols").astype(jnp.int32).reshape(1)
    chip_at = lax.axis_index("rows").astype(jnp.int32).reshape(1)
    swap = [(i, cores - 1 - i) for i in range(cores)]
    parts_count = lax.axis_size("pairs")
    flat = ("pairs", "rows", "cols")
    same_in, same_out, other = [], [], []
    for part in range(parts_count):
        base = part * chips * cores
        for chip in range(chips - 1):
            low = base + chip * cores
            high = low + cores
            same_in += [(low, high), (high + 1, low + 1)]
            same_out += [(high, low), (low + 1, high + 1)]
            other += [(low + 1, high), (high, low + 1)]
        first = base
        last = base + (chips - 1) * cores
        same_in += [(last, last + 1), (first + 1, first)]
        same_out += [(last + 1, last), (first, first + 1)]
        across = (part ^ 1) if parts_count % 2 == 0 else part
        away = (across - part) * chips * cores
        other += [(first, first + away), (last + 1, last + 1 + away)]

    row_shape = shape((2, band, channels), BF)
    params_in = (
        left_image,
        right_image,
        level_zero,
        level_one,
        level_two.transpose(0, 2, 1),
        level_three.transpose(0, 2, 1),
        weight.reshape(3, 3 * channels, features),
    )
    in_hbm = [pltpu.with_memory_space_constraint(x, pltpu.HBM) for x in params_in]
    any_space = pl.BlockSpec(memory_space=pl.ANY)
    level_rows = band * (reach + reach // 2 + reach // 4 + reach // 8) // channels
    level_copies = (reach + reach // 2) // channels + 2 * (band // channels)
    own, near, pack = pl.pallas_call(
        first_kernel,
        out_shape=(row_shape,) * 2 + (shape((4 * band + level_rows, channels), BF),),
        in_specs=[SCALAR] + [any_space] * 6,
        out_specs=vmem(3),
        scratch_shapes=[pltpu.SemaphoreType.DMA((8 + level_copies,))],
        cost_estimate=SMALL,
        compiler_params=params(2),
    )(core, *in_hbm[:6])
    halo_other = lax.ppermute(own, flat, other)
    halo_same = lax.ppermute(near, flat, same_in)
    got = pltpu.with_memory_space_constraint(lax.ppermute(pack, "cols", swap), pltpu.HBM)

    corr, taps = pl.pallas_call(
        local_kernel,
        out_shape=(
            shape((band, reach), BF),
            shape((3 * features, 3 * channels), BF),
        ),
        in_specs=[SCALAR] + [any_space] * 5,
        out_specs=vmem(2),
        scratch_shapes=[
            pltpu.VMEM((3, 3 * channels, features), BF),
            pltpu.VMEM((band, reach), BF),
            pltpu.VMEM((band, reach // 2), BF),
            pltpu.VMEM((reach // 4, band), BF),
            pltpu.VMEM((reach // 8, band), BF),
            pltpu.SemaphoreType.DMA((5,)),
        ],
        cost_estimate=LARGE,
        compiler_params=params(8),
    )(core, in_hbm[6], *in_hbm[2:6])
    own_sum, images_t, skew, skew_t, outer_weight = pl.pallas_call(
        prepare_kernel,
        out_shape=(
            shape((2, size, features), F32),
            shape((2, 2 * channels, size), BF),
            shape((blocks, reach, 2 * reach), BF),
            shape((blocks, 2 * reach, reach), BF),
            shape((3 * channels, features), BF),
        ),
        in_specs=[SCALAR] + [any_space] * 4 + vmem(1),
        out_specs=vmem(5),
        scratch_shapes=[
            pltpu.VMEM((size + 2 * PAD, channels), F32),
            pltpu.VMEM((size, reach), BF),
            pltpu.VMEM((2, 2, size, channels), BF),
            pltpu.VMEM((3, 3 * channels, features), BF),
            pltpu.VMEM((band, reach), BF),
            pltpu.VMEM((band, reach // 2), BF),
            pltpu.VMEM((reach // 4, band), BF),
            pltpu.VMEM((reach // 8, band), BF),
            pltpu.SemaphoreType.DMA((9 + level_copies,)),
        ],
        cost_estimate=SMALL,
        compiler_params=params(12),
    )(core, *in_hbm[:2], got, in_hbm[6], corr)

    piece = features // chips // cores
    tiled = piece % 16 == 0
    wg_shape = (chips, 3 * piece, 3 * channels)
    wg_out = shape(wg_shape if tiled else (3 * features, 3 * channels), F32)
    across_shape = (7 if tiled else 4, max(band, 3 * piece * chips), channels)
    whole_grad, edge_same, edge_other, wg_keep, across = pl.pallas_call(
        functools.partial(main_kernel, chips),
        out_shape=(
            shape((2, size, features), BF),
            pltpu.HBM(row_shape.shape, BF),
            pltpu.HBM(row_shape.shape, BF),
            wg_out,
            shape(across_shape, BF),
        ),
        in_specs=[SCALAR] * 2 + vmem(8),
        out_specs=vmem(1) + [any_space] * 2 + vmem(2),
        scratch_shapes=[
            pltpu.VMEM((size + 2 * PAD, channels), F32),
            pltpu.VMEM((2, size, features), BF),
            pltpu.VMEM((size + 2 * PAD, features), F32),
            pltpu.VMEM((2, size, 3 * features), BF),
            pltpu.VMEM((3 * features, 3 * channels), F32),
            pltpu.VMEM((2, *row_shape.shape), BF),
            pltpu.SemaphoreType.DMA((4,)),
        ],
        cost_estimate=SMALL,
        compiler_params=params(16),
    )(core, chip_at, halo_same, halo_other, outer_weight, own_sum, images_t, skew, skew_t, taps)

    got_other = lax.ppermute(edge_other, flat, other)
    got_same = lax.ppermute(edge_same, flat, same_out)
    across_got = lax.ppermute(across, "cols", swap)
    if tiled:
        chip_wg = pl.pallas_call(
            add_kernel,
            out_shape=shape(wg_shape, BF),
            in_specs=vmem(2),
            out_specs=vmem(1)[0],
            cost_estimate=SMALL,
            compiler_params=params(4),
        )(wg_keep, across_got)
    else:
        halves = wg_keep.reshape(3, chips, cores, piece, 3 * channels).transpose(2, 1, 0, 3, 4)
        halves = halves.reshape(cores, *wg_shape)
        mine = lax.dynamic_index_in_dim(halves, core[0], 0, False)
        theirs = lax.dynamic_index_in_dim(halves, cores - 1 - core[0], 0, False).astype(BF)
        chip_wg = (mine + lax.ppermute(theirs, "cols", swap).astype(F32)).astype(BF)
    parts = lax.all_to_all(chip_wg, "rows", 0, 0, tiled=False)
    grad_left, grad_right, token = pl.pallas_call(
        functools.partial(finish_kernel, chips),
        out_shape=(shape(left_image.shape, BF),) * 2 + (shape((8, 128), F32),),
        in_specs=[SCALAR] * 2 + vmem(5),
        out_specs=vmem(3),
        scratch_shapes=[
            pltpu.VMEM((size + 2 * PAD, features), F32),
            pltpu.VMEM((band + 2 * PAD, features), F32),
        ],
        cost_estimate=LARGE,
        compiler_params=params(8),
    )(core, chip_at, whole_grad, taps, across_got, got_same, got_other)
    scale = 1.0 / math.sqrt(2 * depth * band * chips * cores)
    mine = pl.pallas_call(
        functools.partial(sum_kernel, scale),
        out_shape=shape(wg_shape[1:], F32),
        in_specs=vmem(2),
        out_specs=vmem(1)[0],
        cost_estimate=SMALL,
        compiler_params=params(4),
    )(parts, token)
    theirs = lax.ppermute(mine, "cols", swap)
    if tiled:
        weight_grad = pl.pallas_call(
            finish_weight_kernel,
            out_shape=shape((2 * piece, 9 * channels), F32),
            in_specs=[SCALAR] + vmem(2),
            out_specs=vmem(1)[0],
            cost_estimate=SMALL,
            compiler_params=params(4),
        )(core, mine, theirs)
    else:
        first = core[0] == 0
        both = jnp.stack([jnp.where(first, mine, theirs), jnp.where(first, theirs, mine)])
        both = both.reshape(cores, 3, piece, 3, channels).transpose(0, 2, 3, 1, 4)
        weight_grad = both.reshape(cores * piece, 9 * channels)
    return grad_left, grad_right, weight_grad


def solution(mesh):
    block = P(("pairs", "rows"), "cols", None)
    return jax.shard_map(
        on_device,
        mesh=mesh,
        in_specs=(block, block, P(), block, block, block, block),
        out_specs=(block, block, P(("pairs", "rows"), None)),
        check_vma=False,
    )
```

```python
import functools
import math

import jax
import jax.numpy as jnp
from jax import lax
from jax.experimental import pallas as pl
from jax.experimental.pallas import tpu as pltpu
from jax.sharding import PartitionSpec as P

BF = jnp.bfloat16
F32 = jnp.float32
MIB = 1 << 20
PAD = 8


def dot(a, b):
    return jnp.dot(a, b, preferred_element_type=F32)


def vmem(count):
    return [pl.BlockSpec(memory_space=pltpu.VMEM)] * count


SCALAR = pl.BlockSpec(memory_space=pltpu.SMEM)


def shape(dims, dtype):
    return jax.ShapeDtypeStruct(dims, dtype)


SMALL = pl.CostEstimate(flops=1, bytes_accessed=1, transcendentals=0)


LARGE = pl.CostEstimate(flops=10**11, bytes_accessed=1, transcendentals=0)


def params(mib):
    return pltpu.CompilerParams(vmem_limit_bytes=mib * MIB)


def started(moves, sems):
    copies = [
        pltpu.make_async_copy(source, target, sems.at[index])
        for index, (source, target) in enumerate(moves)
    ]
    for copy in copies:
        copy.start()
    return copies


def packed(source, target, first):
    count, lanes = source.shape[0], target.shape[1]
    moves = []
    for index in range(source.shape[1] // lanes):
        moves.append(
            (source.at[:, pl.ds(index * lanes, lanes)], target.at[pl.ds(first, count)])
        )
        first += count
    return moves, first


def level_moves(levels, pack, first):
    moves = []
    for level in levels:
        more, first = packed(level, pack, first)
        moves += more
    return moves


def first_kernel(core, left, right, own, near, sems):
    c = core[0]
    moves = []
    for image, source in enumerate((left, right)):
        moves += [(source.at[c], own.at[image]), (source.at[1 - c], near.at[image])]
    for copy in started(moves, sems):
        copy.wait()


def pack_kernel(core, left, right, zero, one, two, three, _, pack, sems):
    c = core[0]
    half = left.shape[1]
    moves = []
    for index, source in enumerate((left.at[c], left.at[1 - c], right.at[c], right.at[1 - c])):
        moves.append((source, pack.at[pl.ds(index * half, half)]))
    moves += level_moves([x.at[1 - c] for x in (zero, one, two, three)], pack, 4 * half)
    for copy in started(moves, sems):
        copy.wait()


def spread(factor, reach):
    source = lax.broadcasted_iota(jnp.int32, (reach // factor, reach), 0)
    target = lax.broadcasted_iota(jnp.int32, (reach // factor, reach), 1)
    first = source * factor
    inside = (target >= first) & (target < first + factor)
    return jnp.where(inside, 1.0 / factor, 0.0).astype(BF)


def mirrored(zero, one, two_t, three_t):
    reach = zero.shape[1]
    a = lax.broadcasted_iota(jnp.int32, (reach, reach), 0)
    b = lax.broadcasted_iota(jnp.int32, (reach, reach), 1)
    mirror = jnp.where(a + b == reach - 1, 1.0, 0.0).astype(BF)
    total = zero.astype(F32)
    total = total + dot(one, spread(2, reach))
    total = total + dot(two_t.astype(F32).T.astype(BF), spread(4, reach))
    total = total + dot(three_t.astype(F32).T.astype(BF), spread(8, reach))
    return dot(total.astype(BF), mirror).astype(BF)


def shifted_3(scratch, size, first=0):
    return jnp.concatenate(
        [scratch[pl.ds(PAD + first + by, size)].astype(BF) for by in (-1, 0, 1)], axis=1
    )


def clear_pads(scratch, size):
    zeros = jnp.zeros((PAD, scratch.shape[1]), F32)
    scratch[pl.ds(0, PAD)] = zeros
    scratch[pl.ds(PAD + size, PAD)] = zeros


def local_kernel(
    core, weight_hbm, zero_hbm, one_hbm, two_hbm, three_hbm,
    corr, taps,
    weight, zero, one, two, three, sems,
):
    c = core[0]
    copies = started(
        (
            (weight_hbm, weight),
            (zero_hbm.at[c], zero),
            (one_hbm.at[c], one),
            (two_hbm.at[c], two),
            (three_hbm.at[c], three),
        ),
        sems,
    )
    features = weight.shape[2]
    channels = weight.shape[1] // 3
    copies[0].wait()
    for place, tap in enumerate((2 * c, 1, 2 - 2 * c)):
        for col in range(3):
            piece = weight[tap, pl.ds(col * channels, channels)].astype(F32)
            taps[pl.ds(col * features, features), pl.ds(place * channels, channels)] = (
                piece.T.astype(BF)
            )
    for copy in copies[1:]:
        copy.wait()
    corr[...] = mirrored(zero[...], one[...], two[...], three[...])


def prepare_kernel(
    core, left, right, got, weight_hbm, corr,
    own_sum, images_t, band, band_t, outer_weight,
    padded, rows, images, weight, zero, one, two, three, sems,
):
    c = core[0]
    half = left.shape[1]
    size = 2 * half
    channels = left.shape[2]
    reach = corr.shape[1]
    here = pl.multiple_of(c * half, half)
    there = pl.multiple_of((1 - c) * half, half)
    moves = [(b, a) for a, b in level_moves((zero, one, two, three), got, 4 * half)]
    levels = len(moves)
    for image, mine in enumerate((left, right)):
        for role, row in enumerate((c, 1 - c)):
            block = 2 * image + 1 - role
            moves.append((mine.at[row], images.at[image, role, pl.ds(here, half)]))
            moves.append(
                (got.at[pl.ds(block * half, half)], images.at[image, role, pl.ds(there, half)])
            )
    moves.append((weight_hbm, weight))
    copies = started(moves, sems)
    clear_pads(padded, size)
    rows[pl.ds(here, half)] = corr[...]
    for copy in copies[:levels]:
        copy.wait()
    rows[pl.ds(there, half)] = mirrored(zero[...], one[...], two[...], three[...])
    for copy in copies[levels:]:
        copy.wait()
    for image in range(2):
        total = None
        for role, tap in enumerate((1, 2 - 2 * c)):
            whole = images[image, role].astype(F32)
            padded[pl.ds(PAD, size)] = whole
            images_t[image, pl.ds(role * channels, channels)] = whole.T.astype(BF)
            part = dot(shifted_3(padded, size), weight[tap])
            total = part if total is None else total + part
        own_sum[image] = total
    outer_weight[...] = weight[2 * c]
    for block in range(size // reach):
        values = rows[pl.ds(block * reach, reach)].astype(F32)
        wide = jnp.concatenate([values, jnp.zeros_like(values)], axis=1)
        skewed = pltpu.roll(wide, 1, 1, stride=1, stride_axis=0)
        band[block] = skewed.astype(BF)
        band_t[block] = skewed.T.astype(BF)


def at_end(chips, chip, upper):
    return chip == jnp.where(upper, chips - 1, 0)


def main_kernel(
    chips, core, chip, halo_other, halo_same, weight, own_sum, images_t, band, band_t, taps,
    whole_grad, edge_same, edge_other, wg_keep, across,
    padded, feats, wide, grads, wg, edges, edge_sems,
):
    c = core[0]
    half = halo_same.shape[1]
    size = 2 * half
    channels = halo_same.shape[2]
    features = feats.shape[2]
    blocks, reach = band.shape[0], band.shape[1]
    here = pl.multiple_of(c * half, half)
    there = pl.multiple_of((1 - c) * half, half)
    inverse = 1.0 / math.sqrt(features)
    alone = at_end(chips, chip[0], c == 1)
    clear_pads(padded, size)
    clear_pads(wide, size)
    halo_t = []
    for image in range(2):
        for place, halo in ((here, halo_same), (there, halo_other)):
            padded[pl.ds(PAD + place, half)] = jnp.where(alone, 0.0, halo[image].astype(F32))
        halo_t.append(padded[pl.ds(PAD, size)].T.astype(BF))
        for block in range(blocks):
            rows = pl.ds(block * reach, reach)
            part = dot(shifted_3(padded, reach, block * reach), weight[...])
            feats[image, rows] = (own_sum[image, rows] + part).astype(BF)
    for image in range(2):
        for block in range(blocks):
            low = pl.ds(block * reach, reach)
            if image == 0:
                total = dot(band[block, :, pl.ds(reach, reach)], feats[1, low])
                if block:
                    total = total + dot(
                        band[block, :, pl.ds(0, reach)], feats[1, pl.ds((block - 1) * reach, reach)]
                    )
            else:
                total = dot(band_t[block, pl.ds(reach, reach)], feats[0, low])
                if block + 1 < blocks:
                    total = total + dot(
                        band_t[block + 1, pl.ds(0, reach)],
                        feats[0, pl.ds((block + 1) * reach, reach)],
                    )
            wide[pl.ds(PAD + block * reach, reach)] = total * inverse
        for index, by in enumerate((1, 0, -1)):
            grads[image, :, pl.ds(index * features, features)] = (
                wide[pl.ds(PAD + by, size)].astype(BF)
            )
        whole_grad[image] = grads[image, :, pl.ds(features, features)]
        padded[pl.ds(PAD, size)] = dot(grads[image], taps[:, pl.ds(0, channels)])
        for index, (place, out) in enumerate(((here, edge_same), (there, edge_other))):
            edges[index, image] = padded[pl.ds(PAD + place, half)].astype(BF)
            pltpu.make_async_copy(
                edges.at[index, image], out.at[image], edge_sems.at[2 * image + index]
            ).start()
    inner = dot(images_t[0], grads[0]) + dot(images_t[1], grads[1])
    outer = dot(halo_t[0], grads[0]) + dot(halo_t[1], grads[1])
    for image in range(2):
        for index, out in enumerate((edge_same, edge_other)):
            pltpu.make_async_copy(
                edges.at[index, image], out.at[image], edge_sems.at[2 * image + index]
            ).wait()
    own_wg = inner[:channels].T
    inner_wg = inner[channels:].T
    outer_wg = outer.T
    first = c == 0
    wg[:, pl.ds(0, channels)] = jnp.where(first, outer_wg, inner_wg)
    wg[:, pl.ds(channels, channels)] = own_wg
    wg[:, pl.ds(2 * channels, channels)] = jnp.where(first, inner_wg, outer_wg)
    for image in range(2):
        pair = dot(grads[image, pl.ds(there, half)], taps[:, pl.ds(channels, 2 * channels)])
        for role, row in ((0, c), (1, 1 - c)):
            across[2 * image + row] = pair[:, role * channels : (role + 1) * channels].astype(BF)
    if wg_keep.shape == wg.shape:
        wg_keep[...] = wg[...]
        return
    chunks = wg_keep.shape[0]
    piece = features // chunks // 2
    for col in range(3):
        for chunk in range(chunks):
            start = col * features + chunk * 2 * piece
            wg_keep[chunk, pl.ds(col * piece, piece)] = wg[
                pl.ds(pl.multiple_of(start + c * piece, piece), piece)
            ]
            other = wg[pl.ds(pl.multiple_of(start + (1 - c) * piece, piece), piece)].astype(BF)
            for tap in range(3):
                across[4 + tap, pl.ds((chunk * 3 + col) * piece, piece)] = (
                    other[:, tap * channels : (tap + 1) * channels]
                )


def add_kernel(keep, across, out):
    chunks, rows, lanes = keep.shape
    for chunk in range(chunks):
        for tap in range(3):
            part = pl.ds(tap * lanes // 3, lanes // 3)
            out[chunk, :, part] = (
                keep[chunk, :, part] + across[4 + tap, pl.ds(chunk * rows, rows)].astype(F32)
            ).astype(BF)


def sum_kernel(scale, parts, _, out):
    total = parts[0].astype(F32)
    for index in range(1, parts.shape[0]):
        total = total + parts[index].astype(F32)
    out[...] = total * scale


def finish_weight_kernel(core, mine, got, out):
    c = core[0]
    piece = mine.shape[0] // 3
    channels = mine.shape[1] // 3
    for source, place in ((mine, c), (got, 1 - c)):
        rows = pl.ds(pl.multiple_of(place * piece, piece), piece)
        for tap in range(3):
            for col in range(3):
                out[rows, pl.ds((tap * 3 + col) * channels, channels)] = source[
                    pl.ds(col * piece, piece), pl.ds(tap * channels, channels)
                ]


def keep_kernel(core, whole_grad, taps, _, out, wide, part):
    c = core[0]
    half, channels = out.shape[1], out.shape[2]
    size = whole_grad.shape[1]
    here = pl.multiple_of(c * half, half)
    clear_pads(wide, size)
    for image in range(2):
        wide[pl.ds(PAD, size)] = whole_grad[image].astype(F32)
        part[...] = wide[pl.ds(here, half + 2 * PAD)]
        grads = jnp.concatenate(
            [part[pl.ds(PAD + by, half)].astype(BF) for by in (1, 0, -1)], axis=1
        )
        pair = dot(grads, taps[:, pl.ds(channels, 2 * channels)])
        for role, row in ((0, c), (1, 1 - c)):
            out[2 * image + row] = pair[:, role * channels : (role + 1) * channels]


def finish_kernel(
    chips, core, chip, keep, across, edge_other, edge_same,
    left, right, token,
):
    c = core[0]
    other_alone = at_end(chips, chip[0], c == 1)
    same_alone = at_end(chips, chip[0], c == 0)
    for image, out in enumerate((left, right)):
        for row, edge, alone in ((c, edge_other, other_alone), (1 - c, edge_same, same_alone)):
            out[row] = (
                keep[2 * image + row]
                + across[2 * image + row].astype(F32)
                + jnp.where(alone, 0.0, edge[image].astype(F32))
            ).astype(BF)
    token[...] = jnp.zeros_like(token)


def on_device(left_image, right_image, weight, level_zero, level_one, level_two, level_three):
    depth, band, channels = left_image.shape
    features = weight.shape[1]
    reach = level_zero.shape[2]
    cores = lax.axis_size("cols")
    chips = lax.axis_size("rows")
    size = band * cores
    blocks = size // reach
    core = lax.axis_index("cols").astype(jnp.int32).reshape(1)
    chip_at = lax.axis_index("rows").astype(jnp.int32).reshape(1)
    swap = [(i, cores - 1 - i) for i in range(cores)]
    parts_count = lax.axis_size("pairs")
    flat = ("pairs", "rows", "cols")
    same_in, same_out, other = [], [], []
    for part in range(parts_count):
        base = part * chips * cores
        for chip in range(chips - 1):
            low = base + chip * cores
            high = low + cores
            same_in += [(low, high), (high + 1, low + 1)]
            same_out += [(high, low), (low + 1, high + 1)]
            other += [(low + 1, high), (high, low + 1)]
        first = base
        last = base + (chips - 1) * cores
        same_in += [(last, last + 1), (first + 1, first)]
        same_out += [(last + 1, last), (first, first + 1)]
        across = (part ^ 1) if parts_count % 2 == 0 else part
        away = (across - part) * chips * cores
        other += [(first, first + away), (last + 1, last + 1 + away)]

    row_shape = shape((2, band, channels), BF)
    params_in = (
        left_image,
        right_image,
        level_zero,
        level_one,
        level_two.transpose(0, 2, 1),
        level_three.transpose(0, 2, 1),
        weight.reshape(3, 3 * channels, features),
    )
    in_hbm = [pltpu.with_memory_space_constraint(x, pltpu.HBM) for x in params_in]
    any_space = pl.BlockSpec(memory_space=pl.ANY)
    level_rows = band * (reach + reach // 2 + reach // 4 + reach // 8) // channels
    level_copies = (reach + reach // 2) // channels + 2 * (band // channels)
    own, near = pl.pallas_call(
        first_kernel,
        out_shape=(row_shape,) * 2,
        in_specs=[SCALAR] + [any_space] * 2,
        out_specs=vmem(2),
        scratch_shapes=[pltpu.SemaphoreType.DMA((4,))],
        cost_estimate=SMALL,
        compiler_params=params(2),
    )(core, *in_hbm[:2])
    pack = pl.pallas_call(
        pack_kernel,
        out_shape=shape((4 * band + level_rows, channels), BF),
        in_specs=[SCALAR] + [any_space] * 7,
        out_specs=vmem(1)[0],
        scratch_shapes=[pltpu.SemaphoreType.DMA((4 + level_copies,))],
        cost_estimate=SMALL,
        compiler_params=params(2),
    )(core, *in_hbm[:6], own)
    halo_other = lax.ppermute(own, flat, other)
    halo_same = lax.ppermute(near, flat, same_in)
    got = pltpu.with_memory_space_constraint(lax.ppermute(pack, "cols", swap), pltpu.HBM)

    corr, taps = pl.pallas_call(
        local_kernel,
        out_shape=(
            shape((band, reach), BF),
            shape((3 * features, 3 * channels), BF),
        ),
        in_specs=[SCALAR] + [any_space] * 5,
        out_specs=vmem(2),
        scratch_shapes=[
            pltpu.VMEM((3, 3 * channels, features), BF),
            pltpu.VMEM((band, reach), BF),
            pltpu.VMEM((band, reach // 2), BF),
            pltpu.VMEM((reach // 4, band), BF),
            pltpu.VMEM((reach // 8, band), BF),
            pltpu.SemaphoreType.DMA((5,)),
        ],
        cost_estimate=LARGE,
        compiler_params=params(8),
    )(core, in_hbm[6], *in_hbm[2:6])
    own_sum, images_t, skew, skew_t, outer_weight = pl.pallas_call(
        prepare_kernel,
        out_shape=(
            shape((2, size, features), F32),
            shape((2, 2 * channels, size), BF),
            shape((blocks, reach, 2 * reach), BF),
            shape((blocks, 2 * reach, reach), BF),
            shape((3 * channels, features), BF),
        ),
        in_specs=[SCALAR] + [any_space] * 4 + vmem(1),
        out_specs=vmem(5),
        scratch_shapes=[
            pltpu.VMEM((size + 2 * PAD, channels), F32),
            pltpu.VMEM((size, reach), BF),
            pltpu.VMEM((2, 2, size, channels), BF),
            pltpu.VMEM((3, 3 * channels, features), BF),
            pltpu.VMEM((band, reach), BF),
            pltpu.VMEM((band, reach // 2), BF),
            pltpu.VMEM((reach // 4, band), BF),
            pltpu.VMEM((reach // 8, band), BF),
            pltpu.SemaphoreType.DMA((9 + level_copies,)),
        ],
        cost_estimate=SMALL,
        compiler_params=params(12),
    )(core, *in_hbm[:2], got, in_hbm[6], corr)

    piece = features // chips // cores
    tiled = piece % 16 == 0
    wg_shape = (chips, 3 * piece, 3 * channels)
    wg_out = shape(wg_shape if tiled else (3 * features, 3 * channels), F32)
    across_shape = (7 if tiled else 4, max(band, 3 * piece * chips), channels)
    whole_grad, edge_same, edge_other, wg_keep, across = pl.pallas_call(
        functools.partial(main_kernel, chips),
        out_shape=(
            shape((2, size, features), BF),
            pltpu.HBM(row_shape.shape, BF),
            pltpu.HBM(row_shape.shape, BF),
            wg_out,
            shape(across_shape, BF),
        ),
        in_specs=[SCALAR] * 2 + vmem(8),
        out_specs=vmem(1) + [any_space] * 2 + vmem(2),
        scratch_shapes=[
            pltpu.VMEM((size + 2 * PAD, channels), F32),
            pltpu.VMEM((2, size, features), BF),
            pltpu.VMEM((size + 2 * PAD, features), F32),
            pltpu.VMEM((2, size, 3 * features), BF),
            pltpu.VMEM((3 * features, 3 * channels), F32),
            pltpu.VMEM((2, *row_shape.shape), BF),
            pltpu.SemaphoreType.DMA((4,)),
        ],
        cost_estimate=SMALL,
        compiler_params=params(16),
    )(core, chip_at, halo_other, halo_same, outer_weight, own_sum, images_t, skew, skew_t, taps)

    got_other = lax.ppermute(edge_other, flat, other)
    got_same = lax.ppermute(edge_same, flat, same_out)
    across_got = lax.ppermute(across, "cols", swap)
    if tiled:
        chip_wg = pl.pallas_call(
            add_kernel,
            out_shape=shape(wg_shape, BF),
            in_specs=vmem(2),
            out_specs=vmem(1)[0],
            cost_estimate=SMALL,
            compiler_params=params(4),
        )(wg_keep, across_got)
    else:
        halves = wg_keep.reshape(3, chips, cores, piece, 3 * channels).transpose(2, 1, 0, 3, 4)
        halves = halves.reshape(cores, *wg_shape)
        mine = lax.dynamic_index_in_dim(halves, core[0], 0, False)
        theirs = lax.dynamic_index_in_dim(halves, cores - 1 - core[0], 0, False).astype(BF)
        chip_wg = (mine + lax.ppermute(theirs, "cols", swap).astype(F32)).astype(BF)
    parts = lax.all_to_all(chip_wg, "rows", 0, 0, tiled=False)
    kept = pl.pallas_call(
        keep_kernel,
        out_shape=shape((4, band, channels), F32),
        in_specs=[SCALAR] + vmem(2) + [any_space],
        out_specs=vmem(1)[0],
        scratch_shapes=[
            pltpu.VMEM((size + 2 * PAD, features), F32),
            pltpu.VMEM((band + 2 * PAD, features), F32),
        ],
        cost_estimate=SMALL,
        compiler_params=params(8),
    )(core, whole_grad, taps, across_got)
    grad_left, grad_right, token = pl.pallas_call(
        functools.partial(finish_kernel, chips),
        out_shape=(shape(left_image.shape, BF),) * 2 + (shape((8, 128), F32),),
        in_specs=[SCALAR] * 2 + vmem(4),
        out_specs=vmem(3),
        cost_estimate=LARGE,
        compiler_params=params(4),
    )(core, chip_at, kept, across_got, got_other, got_same)
    scale = 1.0 / math.sqrt(2 * depth * band * chips * cores)
    mine = pl.pallas_call(
        functools.partial(sum_kernel, scale),
        out_shape=shape(wg_shape[1:], F32),
        in_specs=vmem(2),
        out_specs=vmem(1)[0],
        cost_estimate=SMALL,
        compiler_params=params(4),
    )(parts, token)
    theirs = lax.ppermute(mine, "cols", swap)
    if tiled:
        weight_grad = pl.pallas_call(
            finish_weight_kernel,
            out_shape=shape((2 * piece, 9 * channels), F32),
            in_specs=[SCALAR] + vmem(2),
            out_specs=vmem(1)[0],
            cost_estimate=SMALL,
            compiler_params=params(4),
        )(core, mine, theirs)
    else:
        first = core[0] == 0
        both = jnp.stack([jnp.where(first, mine, theirs), jnp.where(first, theirs, mine)])
        both = both.reshape(cores, 3, piece, 3, channels).transpose(0, 2, 3, 1, 4)
        weight_grad = both.reshape(cores * piece, 9 * channels)
    return grad_left, grad_right, weight_grad


def solution(mesh):
    block = P(("pairs", "rows"), "cols", None)
    return jax.shard_map(
        on_device,
        mesh=mesh,
        in_specs=(block, block, P(), block, block, block, block),
        out_specs=(block, block, P(("pairs", "rows"), None)),
        check_vma=False,
    )
```

```python
import functools
import math

import jax
import jax.numpy as jnp
from jax import lax
from jax.experimental import pallas as pl
from jax.experimental.pallas import tpu as pltpu
from jax.sharding import PartitionSpec as P

BF = jnp.bfloat16
F32 = jnp.float32
MIB = 1 << 20
PAD = 8


def dot(a, b):
    return jnp.dot(a, b, preferred_element_type=F32)


def vmem(count):
    return [pl.BlockSpec(memory_space=pltpu.VMEM)] * count


SCALAR = pl.BlockSpec(memory_space=pltpu.SMEM)


def shape(dims, dtype):
    return jax.ShapeDtypeStruct(dims, dtype)


SMALL = pl.CostEstimate(flops=1, bytes_accessed=1, transcendentals=0)


LARGE = pl.CostEstimate(flops=10**11, bytes_accessed=1, transcendentals=0)


def params(mib):
    return pltpu.CompilerParams(vmem_limit_bytes=mib * MIB)


def started(moves, sems):
    copies = [
        pltpu.make_async_copy(source, target, sems.at[index])
        for index, (source, target) in enumerate(moves)
    ]
    for copy in copies:
        copy.start()
    return copies


def packed(source, target, first):
    count, lanes = source.shape[0], target.shape[1]
    moves = []
    for index in range(source.shape[1] // lanes):
        moves.append(
            (source.at[:, pl.ds(index * lanes, lanes)], target.at[pl.ds(first, count)])
        )
        first += count
    return moves, first


def level_moves(levels, pack, first):
    moves = []
    for level in levels:
        more, first = packed(level, pack, first)
        moves += more
    return moves


def first_kernel(core, left, right, own, near, sems):
    c = core[0]
    moves = []
    for image, source in enumerate((left, right)):
        moves += [(source.at[c], own.at[image]), (source.at[1 - c], near.at[image])]
    for copy in started(moves, sems):
        copy.wait()


def pack_kernel(core, left, right, zero, one, two, three, _, pack, sems):
    c = core[0]
    half = left.shape[1]
    moves = []
    for index, source in enumerate((left.at[c], left.at[1 - c], right.at[c], right.at[1 - c])):
        moves.append((source, pack.at[pl.ds(index * half, half)]))
    moves += level_moves([x.at[1 - c] for x in (zero, one, two, three)], pack, 4 * half)
    for copy in started(moves, sems):
        copy.wait()


def spread(factor, reach):
    source = lax.broadcasted_iota(jnp.int32, (reach // factor, reach), 0)
    target = lax.broadcasted_iota(jnp.int32, (reach // factor, reach), 1)
    first = source * factor
    inside = (target >= first) & (target < first + factor)
    return jnp.where(inside, 1.0 / factor, 0.0).astype(BF)


def mirrored(zero, one, two_t, three_t):
    reach = zero.shape[1]
    a = lax.broadcasted_iota(jnp.int32, (reach, reach), 0)
    b = lax.broadcasted_iota(jnp.int32, (reach, reach), 1)
    mirror = jnp.where(a + b == reach - 1, 1.0, 0.0).astype(BF)
    total = zero.astype(F32)
    total = total + dot(one, spread(2, reach))
    total = total + dot(two_t.astype(F32).T.astype(BF), spread(4, reach))
    total = total + dot(three_t.astype(F32).T.astype(BF), spread(8, reach))
    return dot(total.astype(BF), mirror).astype(BF)


def shifted_3(scratch, size, first=0):
    return jnp.concatenate(
        [scratch[pl.ds(PAD + first + by, size)].astype(BF) for by in (-1, 0, 1)], axis=1
    )


def clear_pads(scratch, size):
    zeros = jnp.zeros((PAD, scratch.shape[1]), F32)
    scratch[pl.ds(0, PAD)] = zeros
    scratch[pl.ds(PAD + size, PAD)] = zeros


def local_kernel(
    core, weight_hbm, zero_hbm, one_hbm, two_hbm, three_hbm,
    corr, taps,
    weight, zero, one, two, three, sems,
):
    c = core[0]
    copies = started(
        (
            (weight_hbm, weight),
            (zero_hbm.at[c], zero),
            (one_hbm.at[c], one),
            (two_hbm.at[c], two),
            (three_hbm.at[c], three),
        ),
        sems,
    )
    features = weight.shape[2]
    channels = weight.shape[1] // 3
    copies[0].wait()
    for place, tap in enumerate((2 * c, 1, 2 - 2 * c)):
        for col in range(3):
            piece = weight[tap, pl.ds(col * channels, channels)].astype(F32)
            taps[pl.ds(col * features, features), pl.ds(place * channels, channels)] = (
                piece.T.astype(BF)
            )
    for copy in copies[1:]:
        copy.wait()
    corr[...] = mirrored(zero[...], one[...], two[...], three[...])


def prepare_kernel(
    core, left, right, got, weight_hbm, corr,
    own_sum, images_t, band, band_t, outer_weight,
    padded, rows, images, weight, zero, one, two, three, sems,
):
    c = core[0]
    half = left.shape[1]
    size = 2 * half
    channels = left.shape[2]
    reach = corr.shape[1]
    here = pl.multiple_of(c * half, half)
    there = pl.multiple_of((1 - c) * half, half)
    moves = [(b, a) for a, b in level_moves((zero, one, two, three), got, 4 * half)]
    levels = len(moves)
    for image, mine in enumerate((left, right)):
        for role, row in enumerate((c, 1 - c)):
            block = 2 * image + 1 - role
            moves.append((mine.at[row], images.at[image, role, pl.ds(here, half)]))
            moves.append(
                (got.at[pl.ds(block * half, half)], images.at[image, role, pl.ds(there, half)])
            )
    moves.append((weight_hbm, weight))
    copies = started(moves, sems)
    clear_pads(padded, size)
    rows[pl.ds(here, half)] = corr[...]
    for copy in copies[:levels]:
        copy.wait()
    rows[pl.ds(there, half)] = mirrored(zero[...], one[...], two[...], three[...])
    for copy in copies[levels:]:
        copy.wait()
    for image in range(2):
        total = None
        for role, tap in enumerate((1, 2 - 2 * c)):
            whole = images[image, role].astype(F32)
            padded[pl.ds(PAD, size)] = whole
            images_t[image, pl.ds(role * channels, channels)] = whole.T.astype(BF)
            part = dot(shifted_3(padded, size), weight[tap])
            total = part if total is None else total + part
        own_sum[image] = total
    outer_weight[...] = weight[2 * c]
    for block in range(size // reach):
        values = rows[pl.ds(block * reach, reach)].astype(F32)
        wide = jnp.concatenate([values, jnp.zeros_like(values)], axis=1)
        skewed = pltpu.roll(wide, 1, 1, stride=1, stride_axis=0)
        band[block] = skewed.astype(BF)
        band_t[block] = skewed.T.astype(BF)


def at_end(chips, chip, upper):
    return chip == jnp.where(upper, chips - 1, 0)


def main_kernel(
    chips, core, chip, halo_other, halo_same, weight, own_sum, images_t, band, band_t, taps,
    whole_grad, edge_same, edge_other, wg_keep, across,
    padded, feats, wide, grads, wg, edges, edge_sems,
):
    c = core[0]
    half = halo_same.shape[1]
    size = 2 * half
    channels = halo_same.shape[2]
    features = feats.shape[2]
    blocks, reach = band.shape[0], band.shape[1]
    here = pl.multiple_of(c * half, half)
    there = pl.multiple_of((1 - c) * half, half)
    inverse = 1.0 / math.sqrt(features)
    alone = at_end(chips, chip[0], c == 1)
    clear_pads(padded, size)
    clear_pads(wide, size)
    halo_t = []
    for image in range(2):
        for place, halo in ((here, halo_same), (there, halo_other)):
            padded[pl.ds(PAD + place, half)] = jnp.where(alone, 0.0, halo[image].astype(F32))
        halo_t.append(padded[pl.ds(PAD, size)].T.astype(BF))
        for block in range(blocks):
            rows = pl.ds(block * reach, reach)
            part = dot(shifted_3(padded, reach, block * reach), weight[...])
            feats[image, rows] = (own_sum[image, rows] + part).astype(BF)
    for image in range(2):
        for block in range(blocks):
            low = pl.ds(block * reach, reach)
            if image == 0:
                total = dot(band[block, :, pl.ds(reach, reach)], feats[1, low])
                if block:
                    total = total + dot(
                        band[block, :, pl.ds(0, reach)], feats[1, pl.ds((block - 1) * reach, reach)]
                    )
            else:
                total = dot(band_t[block, pl.ds(reach, reach)], feats[0, low])
                if block + 1 < blocks:
                    total = total + dot(
                        band_t[block + 1, pl.ds(0, reach)],
                        feats[0, pl.ds((block + 1) * reach, reach)],
                    )
            wide[pl.ds(PAD + block * reach, reach)] = total * inverse
        for index, by in enumerate((1, 0, -1)):
            grads[image, :, pl.ds(index * features, features)] = (
                wide[pl.ds(PAD + by, size)].astype(BF)
            )
        whole_grad[image] = grads[image, :, pl.ds(features, features)]
        padded[pl.ds(PAD, size)] = dot(grads[image], taps[:, pl.ds(0, channels)])
        for index, (place, out) in enumerate(((here, edge_same), (there, edge_other))):
            edges[index, image] = padded[pl.ds(PAD + place, half)].astype(BF)
            pltpu.make_async_copy(
                edges.at[index, image], out.at[image], edge_sems.at[2 * image + index]
            ).start()
    inner = dot(images_t[0], grads[0]) + dot(images_t[1], grads[1])
    outer = dot(halo_t[0], grads[0]) + dot(halo_t[1], grads[1])
    for image in range(2):
        for index, out in enumerate((edge_same, edge_other)):
            pltpu.make_async_copy(
                edges.at[index, image], out.at[image], edge_sems.at[2 * image + index]
            ).wait()
    own_wg = inner[:channels].T
    inner_wg = inner[channels:].T
    outer_wg = outer.T
    first = c == 0
    wg[:, pl.ds(0, channels)] = jnp.where(first, outer_wg, inner_wg)
    wg[:, pl.ds(channels, channels)] = own_wg
    wg[:, pl.ds(2 * channels, channels)] = jnp.where(first, inner_wg, outer_wg)
    for image in range(2):
        pair = dot(grads[image, pl.ds(there, half)], taps[:, pl.ds(channels, 2 * channels)])
        for role, row in ((0, c), (1, 1 - c)):
            across[2 * image + row] = pair[:, role * channels : (role + 1) * channels].astype(BF)
    if wg_keep.shape == wg.shape:
        wg_keep[...] = wg[...]
        return
    chunks = wg_keep.shape[0]
    piece = features // chunks // 2
    for col in range(3):
        for chunk in range(chunks):
            start = col * features + chunk * 2 * piece
            wg_keep[chunk, pl.ds(col * piece, piece)] = wg[
                pl.ds(pl.multiple_of(start + c * piece, piece), piece)
            ]
            other = wg[pl.ds(pl.multiple_of(start + (1 - c) * piece, piece), piece)].astype(BF)
            for tap in range(3):
                across[4 + tap, pl.ds((chunk * 3 + col) * piece, piece)] = (
                    other[:, tap * channels : (tap + 1) * channels]
                )


def add_kernel(keep, across, target, out, sems):
    chunks, rows, lanes = keep.shape
    for chunk in range(chunks):
        for tap in range(3):
            part = pl.ds(tap * lanes // 3, lanes // 3)
            out[chunk, :, part] = (
                keep[chunk, :, part] + across[4 + tap, pl.ds(chunk * rows, rows)].astype(F32)
            ).astype(BF)
        pltpu.make_async_copy(out.at[chunk], target.at[chunk], sems.at[chunk]).start()
    for chunk in range(chunks):
        pltpu.make_async_copy(out.at[chunk], target.at[chunk], sems.at[chunk]).wait()


def sum_kernel(scale, parts, _, out):
    total = parts[0].astype(F32)
    for index in range(1, parts.shape[0]):
        total = total + parts[index].astype(F32)
    out[...] = total * scale


def finish_weight_kernel(core, mine, got, out):
    c = core[0]
    piece = mine.shape[0] // 3
    channels = mine.shape[1] // 3
    for source, place in ((mine, c), (got, 1 - c)):
        rows = pl.ds(pl.multiple_of(place * piece, piece), piece)
        for tap in range(3):
            for col in range(3):
                out[rows, pl.ds((tap * 3 + col) * channels, channels)] = source[
                    pl.ds(col * piece, piece), pl.ds(tap * channels, channels)
                ]


def keep_kernel(core, whole_grad, taps, _, out, wide, part):
    c = core[0]
    half, channels = out.shape[1], out.shape[2]
    size = whole_grad.shape[1]
    here = pl.multiple_of(c * half, half)
    clear_pads(wide, size)
    for image in range(2):
        wide[pl.ds(PAD, size)] = whole_grad[image].astype(F32)
        part[...] = wide[pl.ds(here, half + 2 * PAD)]
        grads = jnp.concatenate(
            [part[pl.ds(PAD + by, half)].astype(BF) for by in (1, 0, -1)], axis=1
        )
        pair = dot(grads, taps[:, pl.ds(channels, 2 * channels)])
        for role, row in ((0, c), (1, 1 - c)):
            out[2 * image + row] = pair[:, role * channels : (role + 1) * channels]


def finish_kernel(
    chips, core, chip, keep, across, edge_other, edge_same,
    left, right, token,
    rows, sems,
):
    c = core[0]
    other_alone = at_end(chips, chip[0], c == 1)
    same_alone = at_end(chips, chip[0], c == 0)
    copies = []
    for image, out in enumerate((left, right)):
        for row, edge, alone in ((c, edge_other, other_alone), (1 - c, edge_same, same_alone)):
            index = len(copies)
            rows[index] = (
                keep[2 * image + row]
                + across[2 * image + row].astype(F32)
                + jnp.where(alone, 0.0, edge[image].astype(F32))
            ).astype(BF)
            copies.append(pltpu.make_async_copy(rows.at[index], out.at[row], sems.at[index]))
            copies[-1].start()
    for copy in copies:
        copy.wait()
    token[...] = jnp.zeros_like(token)


def on_device(left_image, right_image, weight, level_zero, level_one, level_two, level_three):
    depth, band, channels = left_image.shape
    features = weight.shape[1]
    reach = level_zero.shape[2]
    cores = lax.axis_size("cols")
    chips = lax.axis_size("rows")
    size = band * cores
    blocks = size // reach
    core = lax.axis_index("cols").astype(jnp.int32).reshape(1)
    chip_at = lax.axis_index("rows").astype(jnp.int32).reshape(1)
    swap = [(i, cores - 1 - i) for i in range(cores)]
    parts_count = lax.axis_size("pairs")
    flat = ("pairs", "rows", "cols")
    same_in, same_out, other = [], [], []
    for part in range(parts_count):
        base = part * chips * cores
        for chip in range(chips - 1):
            low = base + chip * cores
            high = low + cores
            same_in += [(low, high), (high + 1, low + 1)]
            same_out += [(high, low), (low + 1, high + 1)]
            other += [(low + 1, high), (high, low + 1)]
        first = base
        last = base + (chips - 1) * cores
        same_in += [(last, last + 1), (first + 1, first)]
        same_out += [(last + 1, last), (first, first + 1)]
        across = (part ^ 1) if parts_count % 2 == 0 else part
        away = (across - part) * chips * cores
        other += [(first, first + away), (last + 1, last + 1 + away)]

    row_shape = shape((2, band, channels), BF)
    params_in = (
        left_image,
        right_image,
        level_zero,
        level_one,
        level_two.transpose(0, 2, 1),
        level_three.transpose(0, 2, 1),
        weight.reshape(3, 3 * channels, features),
    )
    in_hbm = [pltpu.with_memory_space_constraint(x, pltpu.HBM) for x in params_in]
    any_space = pl.BlockSpec(memory_space=pl.ANY)
    level_rows = band * (reach + reach // 2 + reach // 4 + reach // 8) // channels
    level_copies = (reach + reach // 2) // channels + 2 * (band // channels)
    own, near = pl.pallas_call(
        first_kernel,
        out_shape=(row_shape,) * 2,
        in_specs=[SCALAR] + [any_space] * 2,
        out_specs=vmem(2),
        scratch_shapes=[pltpu.SemaphoreType.DMA((4,))],
        cost_estimate=SMALL,
        compiler_params=params(2),
    )(core, *in_hbm[:2])
    pack = pl.pallas_call(
        pack_kernel,
        out_shape=shape((4 * band + level_rows, channels), BF),
        in_specs=[SCALAR] + [any_space] * 7,
        out_specs=vmem(1)[0],
        scratch_shapes=[pltpu.SemaphoreType.DMA((4 + level_copies,))],
        cost_estimate=SMALL,
        compiler_params=params(2),
    )(core, *in_hbm[:6], own)
    halo_other = lax.ppermute(own, flat, other)
    halo_same = lax.ppermute(near, flat, same_in)
    got = pltpu.with_memory_space_constraint(lax.ppermute(pack, "cols", swap), pltpu.HBM)

    corr, taps = pl.pallas_call(
        local_kernel,
        out_shape=(
            shape((band, reach), BF),
            shape((3 * features, 3 * channels), BF),
        ),
        in_specs=[SCALAR] + [any_space] * 5,
        out_specs=vmem(2),
        scratch_shapes=[
            pltpu.VMEM((3, 3 * channels, features), BF),
            pltpu.VMEM((band, reach), BF),
            pltpu.VMEM((band, reach // 2), BF),
            pltpu.VMEM((reach // 4, band), BF),
            pltpu.VMEM((reach // 8, band), BF),
            pltpu.SemaphoreType.DMA((5,)),
        ],
        cost_estimate=LARGE,
        compiler_params=params(8),
    )(core, in_hbm[6], *in_hbm[2:6])
    own_sum, images_t, skew, skew_t, outer_weight = pl.pallas_call(
        prepare_kernel,
        out_shape=(
            shape((2, size, features), F32),
            shape((2, 2 * channels, size), BF),
            shape((blocks, reach, 2 * reach), BF),
            shape((blocks, 2 * reach, reach), BF),
            shape((3 * channels, features), BF),
        ),
        in_specs=[SCALAR] + [any_space] * 4 + vmem(1),
        out_specs=vmem(5),
        scratch_shapes=[
            pltpu.VMEM((size + 2 * PAD, channels), F32),
            pltpu.VMEM((size, reach), BF),
            pltpu.VMEM((2, 2, size, channels), BF),
            pltpu.VMEM((3, 3 * channels, features), BF),
            pltpu.VMEM((band, reach), BF),
            pltpu.VMEM((band, reach // 2), BF),
            pltpu.VMEM((reach // 4, band), BF),
            pltpu.VMEM((reach // 8, band), BF),
            pltpu.SemaphoreType.DMA((9 + level_copies,)),
        ],
        cost_estimate=SMALL,
        compiler_params=params(12),
    )(core, *in_hbm[:2], got, in_hbm[6], corr)

    piece = features // chips // cores
    tiled = piece % 16 == 0
    wg_shape = (chips, 3 * piece, 3 * channels)
    wg_out = shape(wg_shape if tiled else (3 * features, 3 * channels), F32)
    across_shape = (7 if tiled else 4, max(band, 3 * piece * chips), channels)
    whole_grad, edge_same, edge_other, wg_keep, across = pl.pallas_call(
        functools.partial(main_kernel, chips),
        out_shape=(
            shape((2, size, features), BF),
            pltpu.HBM(row_shape.shape, BF),
            pltpu.HBM(row_shape.shape, BF),
            wg_out,
            shape(across_shape, BF),
        ),
        in_specs=[SCALAR] * 2 + vmem(8),
        out_specs=vmem(1) + [any_space] * 2 + vmem(2),
        scratch_shapes=[
            pltpu.VMEM((size + 2 * PAD, channels), F32),
            pltpu.VMEM((2, size, features), BF),
            pltpu.VMEM((size + 2 * PAD, features), F32),
            pltpu.VMEM((2, size, 3 * features), BF),
            pltpu.VMEM((3 * features, 3 * channels), F32),
            pltpu.VMEM((2, *row_shape.shape), BF),
            pltpu.SemaphoreType.DMA((4,)),
        ],
        cost_estimate=SMALL,
        compiler_params=params(16),
    )(core, chip_at, halo_other, halo_same, outer_weight, own_sum, images_t, skew, skew_t, taps)

    got_other = lax.ppermute(edge_other, flat, other)
    got_same = lax.ppermute(edge_same, flat, same_out)
    across_got = lax.ppermute(across, "cols", swap)
    if tiled:
        chip_wg = pl.pallas_call(
            add_kernel,
            out_shape=pltpu.HBM(wg_shape, BF),
            in_specs=vmem(2),
            out_specs=any_space,
            scratch_shapes=[pltpu.VMEM(wg_shape, BF), pltpu.SemaphoreType.DMA((chips,))],
            cost_estimate=SMALL,
            compiler_params=params(4),
        )(wg_keep, across_got)
    else:
        halves = wg_keep.reshape(3, chips, cores, piece, 3 * channels).transpose(2, 1, 0, 3, 4)
        halves = halves.reshape(cores, *wg_shape)
        mine = lax.dynamic_index_in_dim(halves, core[0], 0, False)
        theirs = lax.dynamic_index_in_dim(halves, cores - 1 - core[0], 0, False).astype(BF)
        chip_wg = (mine + lax.ppermute(theirs, "cols", swap).astype(F32)).astype(BF)
    parts = lax.all_to_all(chip_wg, "rows", 0, 0, tiled=False)
    kept = pl.pallas_call(
        keep_kernel,
        out_shape=shape((4, band, channels), F32),
        in_specs=[SCALAR] + vmem(2) + [any_space],
        out_specs=vmem(1)[0],
        scratch_shapes=[
            pltpu.VMEM((size + 2 * PAD, features), F32),
            pltpu.VMEM((band + 2 * PAD, features), F32),
        ],
        cost_estimate=SMALL,
        compiler_params=params(8),
    )(core, whole_grad, taps, across_got)
    grad_left, grad_right, token = pl.pallas_call(
        functools.partial(finish_kernel, chips),
        out_shape=(pltpu.HBM(left_image.shape, BF),) * 2 + (shape((8, 128), F32),),
        in_specs=[SCALAR] * 2 + vmem(4),
        out_specs=[any_space] * 2 + vmem(1),
        scratch_shapes=[
            pltpu.VMEM((4, band, channels), BF),
            pltpu.SemaphoreType.DMA((4,)),
        ],
        cost_estimate=LARGE,
        compiler_params=params(4),
    )(core, chip_at, kept, across_got, got_other, got_same)
    scale = 1.0 / math.sqrt(2 * depth * band * chips * cores)
    mine = pl.pallas_call(
        functools.partial(sum_kernel, scale),
        out_shape=shape(wg_shape[1:], F32),
        in_specs=vmem(2),
        out_specs=vmem(1)[0],
        cost_estimate=SMALL,
        compiler_params=params(4),
    )(parts, token)
    theirs = lax.ppermute(mine, "cols", swap)
    if tiled:
        weight_grad = pl.pallas_call(
            finish_weight_kernel,
            out_shape=shape((2 * piece, 9 * channels), F32),
            in_specs=[SCALAR] + vmem(2),
            out_specs=vmem(1)[0],
            cost_estimate=SMALL,
            compiler_params=params(4),
        )(core, mine, theirs)
    else:
        first = core[0] == 0
        both = jnp.stack([jnp.where(first, mine, theirs), jnp.where(first, theirs, mine)])
        both = both.reshape(cores, 3, piece, 3, channels).transpose(0, 2, 3, 1, 4)
        weight_grad = both.reshape(cores * piece, 9 * channels)
    return grad_left, grad_right, weight_grad


def solution(mesh):
    block = P(("pairs", "rows"), "cols", None)
    return jax.shard_map(
        on_device,
        mesh=mesh,
        in_specs=(block, block, P(), block, block, block, block),
        out_specs=(block, block, P(("pairs", "rows"), None)),
        check_vma=False,
    )
```
